512 devices in a mesh: group: 4 (over z_hi), ctx: 8 (over y), sample: 16 (over z_lo, x, core).
Axes of the slice: x: 4, y: 8, z: 8 (z_hi: 4, z_lo: 2; z = z_hi * 2 + z_lo), core: 2. Of those that a mesh axis runs over, the one named last changes fastest.
Arguments:
- q_nope: bfloat16 [8192, 16384], P(('group', 'sample'), 'ctx'), parts along dimension 0, may hold values from -6 to 6
- q_rope: bfloat16 [8192, 8192], P(('group', 'sample'), 'ctx'), parts along dimension 0, may hold values from -400 to 400
- prompt_latent: bfloat16 [1024, 512], P(('group', 'ctx')), parts along dimension 0, may hold values from -6 to 6
- prompt_rope: bfloat16 [1024, 64], P(('group', 'ctx')), parts along dimension 0, may hold values from -4.5 to 4.5
- resp_latent: bfloat16 [8192, 512], P(('group', 'sample')), parts along dimension 0, may hold values from -6 to 6
- resp_rope: bfloat16 [8192, 64], P(('group', 'sample')), parts along dimension 0, may hold values from -6 to 6
- w_key: bfloat16 [512, 16384], P('sample', 'ctx'), may hold values from -0.25 to 0.25
- w_value: bfloat16 [512, 16384], P('sample', 'ctx'), may hold values from -0.25 to 0.25
- out_grad: bfloat16 [8192, 16384], P(('group', 'sample'), 'ctx'), parts along dimension 0, may hold values from -6 to 6
- lengths: int32 [64], P(('group', 'sample')), parts along dimension 0, may hold values from 16 to 128, as said below
- offsets: int32 [64], P(('group', 'sample')), parts along dimension 0, may hold values from 128 to 256, as said below
Outputs:
- attn_out: bfloat16 [8192, 16384], P(('group', 'sample'), 'ctx'), parts along dimension 0
- grad_query_nope: bfloat16 [8192, 16384], P(('group', 'sample'), 'ctx'), parts along dimension 0
- grad_query_rope: bfloat16 [8192, 8192], P(('group', 'sample'), 'ctx'), parts along dimension 0
- grad_prompt_latent: float32 [1024, 512], P(('group', 'ctx')), parts along dimension 0
- grad_prompt_rope: float32 [1024, 64], P(('group', 'ctx')), parts along dimension 0
- grad_resp_latent: float32 [8192, 512], P(('group', 'sample')), parts along dimension 0
- grad_resp_rope: float32 [8192, 64], P(('group', 'sample')), parts along dimension 0
The draws below stay inside these ranges and needn't reach their ends.
There are 4 independent parts, one for each index of `group`. The reference program is written for one: setup_inputs(seed, part) draws one part's arguments, and reference() takes and returns one part's arrays. A program takes and returns all parts, laid end to end along the dimension named above; an argument that names none is the same for every part. Nothing has to cross between parts.
Inputs may be any that keep to these rules, and one draw needn't show every extreme that they name: `lengths`: one response has exactly 128 live slots and one exactly 16. `offsets`: one response follows all 256 prompt rows and one exactly 128.
All inputs are finite; a program needn't handle non-finite values.
Results may differ from the reference program's by a relative error of at most 0.017.
Values may be sent and summed in bfloat16 or wider, within the bound.
No kernel may reach another device: no remote copies, remote signals or barrier semaphores. Data moves between devices by JAX's collectives and lax.ppermute only.
A program may use at most 64 MiB of HBM per device.

```python
import math
import jax
import jax.numpy as jnp
from jax import lax

HEADS = 128
LATENT = 512
ROPE_DIM = 64
NOPE_DIM = 128
V_DIM = 128
PROMPT = 256
RESP_MAX = 128
SAMPLES = 16
RESP_ROWS = 2048


def rope_pair(key, strength):
    key_query, key_prompt, key_select, key_target = jax.random.split(key, 4)
    row_total = SAMPLES * RESP_MAX
    quarter = PROMPT // 4
    prompt_keys = jnp.clip(jax.random.normal(key_prompt, (PROMPT, ROPE_DIM), jnp.float32), -4.5, 4.5)
    base_queries = jnp.clip(jax.random.normal(key_query, (row_total, HEADS, ROPE_DIM), jnp.float32), -4.5, 4.5)
    target = jax.random.randint(key_target, (row_total,), 0, quarter)
    chosen = (jax.random.uniform(key_select, (row_total,)) < 0.03).astype(jnp.float32) * strength
    match_table = (target[:, None] == jnp.arange(quarter)[None, :]).astype(jnp.float32) * chosen[:, None]
    hit_rows = jnp.max(match_table, axis=0)
    lower_rows = prompt_keys[:quarter]
    upper_rows = prompt_keys[quarter:2 * quarter]
    upper_rows = upper_rows + hit_rows[:, None] * (0.99 * lower_rows - upper_rows)
    prompt_keys = jnp.concatenate([lower_rows, upper_rows, prompt_keys[2 * quarter:]], axis=0)
    queries = base_queries
    return (queries.reshape(row_total, HEADS * ROPE_DIM), prompt_keys)


def draw_q_rope(key, part):
    strength = 0.0
    queries, prompt_keys = rope_pair(key, strength)
    return queries.astype(jnp.bfloat16)


def draw_prompt_rope(key, part):
    strength = 0.0
    queries, prompt_keys = rope_pair(key, strength)
    return prompt_keys.astype(jnp.bfloat16)


def draw_lengths(key, part):
    key = jax.random.fold_in(key, 11)
    key_values, key_order = jax.random.split(key)
    lowest = RESP_MAX // 8
    values = jax.random.randint(key_values, (SAMPLES,), lowest, RESP_MAX + 1)
    order = jax.random.permutation(key_order, SAMPLES)
    values = values.at[order[0]].set(RESP_MAX).at[order[1]].set(lowest)
    return values.astype(jnp.int32)


def draw_offsets(key, part):
    key = jax.random.fold_in(key, 12)
    key_values, key_order = jax.random.split(key)
    lowest = PROMPT // 2
    values = jax.random.randint(key_values, (SAMPLES,), lowest, PROMPT + 1)
    order = jax.random.permutation(key_order, SAMPLES)
    values = values.at[order[0]].set(PROMPT).at[order[1]].set(lowest)
    return values.astype(jnp.int32)


def block_scale(stream_key, extent, shards, least, top_value):
    gain, own = 1.0, jax.random.fold_in(stream_key, 6)
    for axis_at, shards_of in shards:
        steps = jnp.exp(jax.random.uniform(jax.random.fold_in(own, axis_at), (shards_of,), jnp.float32, least / len(shards), top_value / len(shards)))
        gain = gain * jnp.repeat(steps, extent[axis_at] // shards_of).reshape([-1 if axis == axis_at else 1 for axis in range(len(extent))])
    return gain


def scatter_about(stream_key, extent, deviation, most, cuts=(), held_as=jnp.bfloat16):
    values = deviation * jax.random.normal(stream_key, extent, jnp.float32)
    if cuts:
        values = values * block_scale(stream_key, extent, cuts, -0.22, 0.18)
    return jnp.clip(values, -most, most).astype(held_as)


def setup_inputs(seed: int = 0, part: int = 0) -> dict:
    splits = jax.random.split(jax.random.key(seed), 12)
    own_keys = jax.random.split(jax.random.fold_in(splits[11], part), 12)
    q_nope = scatter_about(own_keys[0], (RESP_ROWS, HEADS * NOPE_DIM), 1.0, 6.0, ((0, 16), (1, 8)))
    q_rope = draw_q_rope(jax.random.fold_in(jax.random.fold_in(splits[11], part), 71), part)
    prompt_latent = scatter_about(own_keys[2], (PROMPT, LATENT), 1.0, 6.0, ((0, 8),))
    prompt_rope = draw_prompt_rope(jax.random.fold_in(jax.random.fold_in(splits[11], part), 71), part)
    resp_latent = scatter_about(own_keys[4], (RESP_ROWS, LATENT), 1.0, 6.0, ((0, 16),))
    resp_rope = scatter_about(own_keys[5], (RESP_ROWS, ROPE_DIM), 1.0, 6.0, ((0, 16),))
    w_key = scatter_about(splits[6], (LATENT, HEADS * NOPE_DIM), LATENT ** -0.5, 0.25, ((0, 16), (1, 8)))
    w_value = scatter_about(splits[7], (LATENT, HEADS * V_DIM), LATENT ** -0.5, 0.25, ((0, 16), (1, 8)))
    out_grad = scatter_about(own_keys[8], (RESP_ROWS, HEADS * V_DIM), 1.0, 6.0, ((0, 16), (1, 8)))
    lengths = draw_lengths(jax.random.fold_in(jax.random.fold_in(splits[11], part), 71), part)
    offsets = draw_offsets(jax.random.fold_in(jax.random.fold_in(splits[11], part), 71), part)
    return dict(q_nope=q_nope, q_rope=q_rope, prompt_latent=prompt_latent, prompt_rope=prompt_rope, resp_latent=resp_latent, resp_rope=resp_rope, w_key=w_key, w_value=w_value, out_grad=out_grad, lengths=lengths, offsets=offsets)


NEG_FILL = -1e+30

def product(pattern, left_side, right_side):
    return jnp.einsum(pattern, left_side.astype(jnp.float32), right_side.astype(jnp.float32))

def one_sample(query_nope, query_rope, grad_out, resp_lat, resp_rot, length, offset, prompt_latent, prompt_rope, key_proj, value_proj):
    row_count = query_nope.shape[0]
    prompt_count = prompt_latent.shape[0]
    keys_lat = jnp.concatenate([prompt_latent, resp_lat], axis=0)
    keys_rot = jnp.concatenate([prompt_rope, resp_rot], axis=0)
    slot_index = jnp.arange(row_count, dtype=jnp.int32)
    key_index = jnp.arange(prompt_count + row_count, dtype=jnp.int32)
    live_rows = slot_index < length
    visible = jnp.where(key_index[None, :] < prompt_count, key_index[None, :] < offset, key_index[None, :] - prompt_count <= slot_index[:, None])
    score_scale = 1.0 / math.sqrt(NOPE_DIM + ROPE_DIM)
    absorbed = product('rhn,lhn->rhl', query_nope, key_proj).astype(jnp.bfloat16)
    scores = (product('rhl,kl->rhk', absorbed, keys_lat) + product('rhe,ke->rhk', query_rope, keys_rot)) * score_scale
    scores = jnp.where(visible[:, None, :], scores, NEG_FILL)
    row_max = lax.optimization_barrier(jnp.max(scores, axis=-1, keepdims=True))
    raised = jnp.exp(scores - row_max)
    probability = raised / lax.optimization_barrier(jnp.sum(raised, axis=-1, keepdims=True))
    prob_half = probability.astype(jnp.bfloat16)
    latent_out = product('rhk,kl->rhl', prob_half, keys_lat).astype(jnp.bfloat16)
    projected = product('rhl,lhv->rhv', latent_out, value_proj)
    attn_rows = jnp.where(live_rows[:, None, None], projected, 0.0).astype(jnp.bfloat16)
    grad_rows = jnp.where(live_rows[:, None, None], grad_out, jnp.zeros_like(grad_out))
    grad_latent = product('rhv,lhv->rhl', grad_rows, value_proj).astype(jnp.bfloat16)
    grad_probs = product('rhl,kl->rhk', grad_latent, keys_lat)
    inner_sum = lax.optimization_barrier(jnp.sum(probability * grad_probs, axis=-1, keepdims=True))
    grad_scores = (probability * (grad_probs - inner_sum) * score_scale).astype(jnp.bfloat16)
    grad_absorbed = product('rhk,kl->rhl', grad_scores, keys_lat).astype(jnp.bfloat16)
    grad_qrot = product('rhk,ke->rhe', grad_scores, keys_rot).astype(jnp.bfloat16)
    grad_qnope = product('rhl,lhn->rhn', grad_absorbed, key_proj).astype(jnp.bfloat16)
    grad_keys_lat = product('rhk,rhl->kl', grad_scores, absorbed) + product('rhk,rhl->kl', prob_half, grad_latent)
    grad_keys_rot = product('rhk,rhe->ke', grad_scores, query_rope)
    return (attn_rows, grad_qnope, grad_qrot, grad_keys_lat[:prompt_count], grad_keys_rot[:prompt_count], grad_keys_lat[prompt_count:], grad_keys_rot[prompt_count:])

def reference(q_nope, q_rope, prompt_latent, prompt_rope, resp_latent, resp_rope, w_key, w_value, out_grad, lengths, offsets):
    key_proj = w_key.reshape(LATENT, HEADS, NOPE_DIM)
    value_proj = w_value.reshape(LATENT, HEADS, V_DIM)
    stacked = (q_nope.reshape(SAMPLES, RESP_MAX, HEADS, NOPE_DIM), q_rope.reshape(SAMPLES, RESP_MAX, HEADS, ROPE_DIM), out_grad.reshape(SAMPLES, RESP_MAX, HEADS, V_DIM), resp_latent.reshape(SAMPLES, RESP_MAX, LATENT), resp_rope.reshape(SAMPLES, RESP_MAX, ROPE_DIM), lengths, offsets)

    def step_sample(running, inputs):
        results = one_sample(inputs[0], inputs[1], inputs[2], inputs[3], inputs[4], inputs[5], inputs[6], prompt_latent, prompt_rope, key_proj, value_proj)
        totals = (running[0] + results[3], running[1] + results[4])
        return (totals, (results[0], results[1], results[2], results[5], results[6]))
    start_sums = (jnp.zeros((PROMPT, LATENT), jnp.float32), jnp.zeros((PROMPT, ROPE_DIM), jnp.float32))
    prompt_sums, stacked_out = lax.scan(step_sample, start_sums, stacked)
    attn_out = stacked_out[0].reshape(RESP_ROWS, HEADS * V_DIM)
    grad_query_nope = stacked_out[1].reshape(RESP_ROWS, HEADS * NOPE_DIM)
    grad_query_rope = stacked_out[2].reshape(RESP_ROWS, HEADS * ROPE_DIM)
    grad_resp_latent = stacked_out[3].reshape(RESP_ROWS, LATENT)
    grad_resp_rope = stacked_out[4].reshape(RESP_ROWS, ROPE_DIM)
    return (attn_out, grad_query_nope, grad_query_rope, prompt_sums[0], prompt_sums[1], grad_resp_latent, grad_resp_rope)
```

```python
import math

import jax
import jax.numpy as jnp
from jax import lax
from jax.experimental import pallas as pl
from jax.experimental.pallas import tpu as pltpu
from jax.sharding import PartitionSpec as P

NEG_FILL = -1e30
HEADS_PER_STEP = 4
LAT = 512
WIDE = 640
BF = jnp.bfloat16
F32 = jnp.float32


def spread_weights(w_key, w_value, copies):
    rows, cols = w_key.shape

    def kernel(key_ref, value_ref, out_ref, sems):
        moves = []
        for j in range(copies):
            moves.append(pltpu.make_async_copy(key_ref, out_ref.at[j, pl.ds(0, rows)], sems.at[2 * j]))
            moves.append(pltpu.make_async_copy(value_ref, out_ref.at[j, pl.ds(rows, rows)], sems.at[2 * j + 1]))
        for move in moves:
            move.start()
        for move in moves:
            move.wait()

    return pl.pallas_call(
        kernel,
        out_shape=pltpu.HBM((copies, 2 * rows, cols), BF),
        in_specs=[pl.BlockSpec(memory_space=pltpu.VMEM)] * 2,
        out_specs=pl.BlockSpec(memory_space=pl.ANY),
        scratch_shapes=[pltpu.SemaphoreType.DMA((2 * copies,))],
        name="spread_weights",
    )(w_key, w_value)


def dot(left, right, dims):
    return lax.dot_general(left, right, (dims, ((), ())), preferred_element_type=F32)


def attention(facts, q_nope, q_rope, out_grad, keys, w_own, w_other):
    row_count = q_nope.shape[0]
    key_count = keys.shape[0]
    prompt_count = key_count - row_count
    head_count = q_nope.shape[1] // 128
    hps = HEADS_PER_STEP
    steps = head_count // hps
    chips, two_rows, _ = w_own.shape
    w_rows = two_rows // 2
    ctx_count = 8
    owned = prompt_count // ctx_count
    resp_owned = row_count // ctx_count
    scale = 1.0 / math.sqrt(192.0)
    exp_scale = scale * math.log2(math.e)

    def kernel(facts_ref, qn_ref, qr_ref, og_ref, keys_ref, wk_own, wv_own, wk_oth, wv_oth,
               out_ref, gqn_ref, gqr_ref, prompt_ref, resp_ref, w_all, bias, live, acc, acc_rope):
        step = pl.program_id(0)
        length, offset, ctx, core = facts_ref[0], facts_ref[1], facts_ref[2], facts_ref[3]

        @pl.when(step == 0)
        def _():
            key = lax.broadcasted_iota(jnp.int32, (key_count, row_count), 0)
            slot = lax.broadcasted_iota(jnp.int32, (key_count, row_count), 1)
            block = lax.shift_right_logical(key, 5)
            place = jnp.bitwise_xor(block, ctx) * owned + jnp.bitwise_and(key, owned - 1)
            bias[...] = jnp.where(
                key < prompt_count,
                jnp.where(place < offset, 0.0, NEG_FILL),
                jnp.where(key - prompt_count <= slot, 0.0, NEG_FILL))
            row = lax.broadcasted_iota(jnp.int32, (row_count, 128), 0)
            live[...] = jnp.where(row < length, 1.0, 0.0)
            acc[...] = jnp.zeros_like(acc)
            acc_rope[...] = jnp.zeros_like(acc_rope)

        for j in range(chips):
            own_at = pl.ds(pl.multiple_of(j * 2 * w_rows + core * w_rows, w_rows), w_rows)
            oth_at = pl.ds(pl.multiple_of(j * 2 * w_rows + (1 - core) * w_rows, w_rows), w_rows)
            for h in range(hps):
                src = slice(128 * h, 128 * h + 128)
                w_all[own_at, 256 * h:256 * h + 128] = wk_own[j, :, src]
                w_all[own_at, 256 * h + 128:256 * h + 256] = wv_own[j, :, src]
                w_all[oth_at, 256 * h:256 * h + 128] = wk_oth[j, :, src]
                w_all[oth_at, 256 * h + 128:256 * h + 256] = wv_oth[j, :, src]

        keys_lat = keys_ref[:, :LAT]
        keys_rot = keys_ref[:, LAT:]
        alive = live[...]
        lane = lax.broadcasted_iota(jnp.int32, (row_count, 128), 1)
        grads = []
        rope_pair = []
        rope_sum = None
        for h in range(hps):
            col = slice(128 * h, 128 * h + 128)
            both = dot(keys_lat, w_all[:, 256 * h:256 * h + 256], ((1,), (0,))).astype(BF)
            value = both[:, 128:]
            key_full = jnp.concatenate([both[:, :128], keys_rot], axis=1)
            mine = (lane < 64) if h % 2 == 0 else (lane >= 64)
            rope = jnp.where(mine, qr_ref[:, 128 * (h // 2):128 * (h // 2) + 128].astype(F32), 0.0).astype(BF)
            query = jnp.concatenate([qn_ref[:, col], rope], axis=1)
            grad_out = (og_ref[:, col].astype(F32) * alive).astype(BF)
            scores = dot(key_full, query, ((1,), (1,))) + bias[...]
            top = jnp.max(scores, axis=0, keepdims=True)
            raised = jnp.exp2((scores - top) * exp_scale)
            prob = raised * (1.0 / jnp.sum(raised, axis=0, keepdims=True))
            prob_half = prob.astype(BF)
            grad_prob = dot(value, grad_out, ((1,), (1,)))
            weighed = prob * grad_prob
            inner = jnp.sum(weighed, axis=0, keepdims=True)
            grad_score = ((weighed - prob * inner) * scale).astype(BF)
            attn = dot(prob_half, value, ((0,), (0,)))
            out_ref[:, col] = (attn * alive).astype(BF)
            grad_query = dot(grad_score, key_full, ((0,), (0,)))
            gqn_ref[:, col] = grad_query[:, :128].astype(BF)
            rope_pair.append(grad_query[:, 128:])
            if h % 2 == 1:
                gqr_ref[:, 128 * (h // 2):128 * (h // 2) + 128] = jnp.where(
                    lane < 64, rope_pair[h - 1], rope_pair[h]).astype(BF)
            grad_key = dot(grad_score, query, ((1,), (0,)))
            grad_value = dot(prob_half, grad_out, ((1,), (0,)))
            grads += [grad_key[:, :128].astype(BF), grad_value.astype(BF)]
            rope_sum = grad_key[:, 128:] if rope_sum is None else rope_sum + grad_key[:, 128:]
        acc[...] += dot(jnp.concatenate(grads, axis=1), w_all[...], ((1,), (1,)))
        acc_rope[...] += rope_sum

        @pl.when(step == steps - 1)
        def _():
            for owner in range(ctx_count):
                at = pl.ds(pl.multiple_of(jnp.bitwise_xor(ctx, owner) * owned, owned), owned)
                prompt_ref[owner, :, :LAT] = acc[at, :].astype(BF)
                prompt_ref[owner, :, LAT:] = acc_rope[at, :].astype(BF)
                at = slice(prompt_count + owner * resp_owned, prompt_count + (owner + 1) * resp_owned)
                resp_ref[owner, :, :LAT] = acc[at, :].astype(BF)
                resp_ref[owner, :, LAT:] = acc_rope[at, :].astype(BF)

    wide = 128 * hps
    return pl.pallas_call(
        kernel,
        grid=(steps,),
        in_specs=[
            pl.BlockSpec(memory_space=pltpu.SMEM),
            pl.BlockSpec((row_count, wide), lambda i: (0, i)),
            pl.BlockSpec((row_count, wide // 2), lambda i: (0, i)),
            pl.BlockSpec((row_count, wide), lambda i: (0, i)),
            pl.BlockSpec((key_count, WIDE), lambda i: (0, 0)),
            pl.BlockSpec((chips, w_rows, wide), lambda i: (0, 0, i)),
            pl.BlockSpec((chips, w_rows, wide), lambda i: (0, 1, i)),
            pl.BlockSpec((chips, w_rows, wide), lambda i: (0, 0, i)),
            pl.BlockSpec((chips, w_rows, wide), lambda i: (0, 1, i)),
        ],
        out_specs=[
            pl.BlockSpec((row_count, wide), lambda i: (0, i)),
            pl.BlockSpec((row_count, wide), lambda i: (0, i)),
            pl.BlockSpec((row_count, wide // 2), lambda i: (0, i)),
            pl.BlockSpec((ctx_count, owned, WIDE), lambda i: (0, 0, 0)),
            pl.BlockSpec((ctx_count, resp_owned, WIDE), lambda i: (0, 0, 0)),
        ],
        out_shape=[
            jax.ShapeDtypeStruct(q_nope.shape, BF),
            jax.ShapeDtypeStruct(q_nope.shape, BF),
            jax.ShapeDtypeStruct(q_rope.shape, BF),
            pltpu.HBM((ctx_count, owned, WIDE), BF),
            pltpu.HBM((ctx_count, resp_owned, WIDE), BF),
        ],
        scratch_shapes=[
            pltpu.VMEM((LAT, 256 * hps), BF),
            pltpu.VMEM((key_count, row_count), F32),
            pltpu.VMEM((row_count, 128), F32),
            pltpu.VMEM((key_count, LAT), F32),
            pltpu.VMEM((key_count, 128), F32),
        ],
        compiler_params=pltpu.CompilerParams(vmem_limit_bytes=40 * 2**20),
        cost_estimate=pl.CostEstimate(flops=6 * 10**9, bytes_accessed=8 * 2**20, transcendentals=2048 * 384),
        name="attention",
    )(facts, q_nope, q_rope, out_grad, keys, w_own, w_own, w_other, w_other)


def add_resp(terms, prompt_terms):
    def kernel(terms_ref, through_ref, resp_ref, out_ref):
        del through_ref, out_ref
        total = terms_ref[0].astype(F32)
        for j in range(1, terms.shape[0]):
            total = total + terms_ref[j].astype(F32)
        resp_ref[...] = total.astype(BF)

    return pl.pallas_call(
        kernel,
        in_specs=[pl.BlockSpec(memory_space=pltpu.VMEM), pl.BlockSpec(memory_space=pl.ANY)],
        out_specs=[pl.BlockSpec(memory_space=pltpu.VMEM), pl.BlockSpec(memory_space=pl.ANY)],
        out_shape=[
            jax.ShapeDtypeStruct(terms.shape[1:], BF),
            pltpu.HBM(prompt_terms.shape, BF),
        ],
        input_output_aliases={1: 1},
        name="add_resp",
    )(terms, prompt_terms)


def add_prompt(terms, copies):
    owned = terms.shape[1]

    def kernel(terms_ref, prompt_ref, held, sems):
        total = terms_ref[0].astype(F32)
        for j in range(1, terms.shape[0]):
            total = total + terms_ref[j].astype(F32)
        held[...] = total.astype(BF)
        moves = [pltpu.make_async_copy(held, prompt_ref.at[j], sems.at[j]) for j in range(copies)]
        for move in moves:
            move.start()
        for move in moves:
            move.wait()

    return pl.pallas_call(
        kernel,
        in_specs=[pl.BlockSpec(memory_space=pltpu.VMEM)],
        out_specs=pl.BlockSpec(memory_space=pl.ANY),
        out_shape=pltpu.HBM((copies, owned, WIDE), BF),
        scratch_shapes=[pltpu.VMEM((owned, WIDE), BF), pltpu.SemaphoreType.DMA((copies,))],
        name="add_prompt",
    )(terms)


def finish(facts, prompt_terms, resp_sum):
    samples, owned, _ = prompt_terms.shape
    row_count = resp_sum.shape[0]
    resp_owned = row_count // 8

    def kernel(facts_ref, prompt_ref, resp_ref, plat_ref, prot_ref, rlat_ref, rrot_ref, held):
        ctx = facts_ref[2]
        total = prompt_ref[0].astype(F32)
        for j in range(1, samples):
            total = total + prompt_ref[j].astype(F32)
        plat_ref[...] = total[:, :LAT]
        prot_ref[...] = total[:, LAT:LAT + 64] + total[:, LAT + 64:]
        for owner in range(8):
            at = pl.ds(pl.multiple_of(jnp.bitwise_xor(ctx, owner) * resp_owned, resp_owned), resp_owned)
            rows = resp_ref[at, :].astype(F32)
            to = slice(owner * resp_owned, (owner + 1) * resp_owned)
            rlat_ref[to, :] = rows[:, :LAT]
            held[to, :] = rows[:, LAT:]
        turned = jnp.swapaxes(held[...], 0, 1)
        rrot_ref[...] = turned[:64] + turned[64:]

    vm = pl.BlockSpec(memory_space=pltpu.VMEM)
    return pl.pallas_call(
        kernel,
        in_specs=[pl.BlockSpec(memory_space=pltpu.SMEM), vm, vm],
        out_specs=[vm] * 4,
        out_shape=[
            jax.ShapeDtypeStruct((owned, LAT), F32),
            jax.ShapeDtypeStruct((owned, 64), F32),
            jax.ShapeDtypeStruct((row_count, LAT), F32),
            jax.ShapeDtypeStruct((64, row_count), F32),
        ],
        scratch_shapes=[pltpu.VMEM((row_count, 128), F32)],
        name="finish",
    )(facts, prompt_terms, resp_sum)


def butterfly(block, distances=(1, 2, 4)):
    for k in distances:
        block = jnp.concatenate([block, lax.ppermute(block, "ctx", [(i, i ^ k) for i in range(8)])], axis=0)
    return block


def per_device(
    q_nope,
    q_rope,
    prompt_latent,
    prompt_rope,
    resp_latent,
    resp_rope,
    w_key,
    w_value,
    out_grad,
    lengths,
    offsets,
):
    ctx = lax.axis_index("ctx").astype(jnp.int32)
    core = jnp.bitwise_and(lax.axis_index("sample").astype(jnp.int32), 1)
    facts = jnp.concatenate([lengths, offsets, ctx[None], core[None]])
    same_core = [[2 * chip + c for chip in range(8)] for c in range(2)]
    w_own = lax.all_to_all(
        spread_weights(w_key, w_value, 8), "sample", 0, 0, tiled=True, axis_index_groups=same_core)
    prompt_keys = butterfly(jnp.concatenate([prompt_latent, prompt_rope, prompt_rope], axis=1))
    keys = jnp.concatenate(
        [prompt_keys, jnp.concatenate([resp_latent, resp_rope, resp_rope], axis=1)], axis=0)
    w_own, keys = lax.optimization_barrier((w_own, keys))
    w_other = lax.ppermute(w_own, "sample", [(i, i ^ 1) for i in range(16)])
    attn_out, grad_query_nope, grad_query_rope, prompt_terms, resp_terms = attention(
        facts, q_nope, q_rope, out_grad, keys, w_own, w_other)
    resp_terms = lax.all_to_all(resp_terms, "ctx", 0, 0, tiled=True)
    resp_part, prompt_terms = add_resp(resp_terms, prompt_terms)
    prompt_terms = lax.all_to_all(prompt_terms, "ctx", 0, 0, tiled=True)
    resp_half, prompt_terms = lax.optimization_barrier((butterfly(resp_part, (1, 2)), prompt_terms))
    resp_sum = butterfly(resp_half, (4,))
    prompt_part = lax.all_to_all(add_prompt(prompt_terms, 16), "sample", 0, 0, tiled=True)
    prompt_lat, prompt_rot, resp_lat, resp_rot = finish(facts, prompt_part, resp_sum)
    return (attn_out, grad_query_nope, grad_query_rope, prompt_lat, prompt_rot, resp_lat, resp_rot.T)


def solution(mesh):
    placed = (
        P(("group", "sample"), "ctx"),
        P(("group", "sample"), "ctx"),
        P(("group", "ctx"), None),
        P(("group", "ctx"), None),
        P(("group", "sample"), None),
        P(("group", "sample"), None),
        P("sample", "ctx"),
        P("sample", "ctx"),
        P(("group", "sample"), "ctx"),
        P(("group", "sample")),
        P(("group", "sample")),
    )
    return jax.shard_map(
        per_device,
        mesh=mesh,
        in_specs=placed,
        out_specs=(
            P(("group", "sample"), "ctx"),
            P(("group", "sample"), "ctx"),
            P(("group", "sample"), "ctx"),
            P(("group", "ctx"), None),
            P(("group", "ctx"), None),
            P(("group", "sample"), None),
            P(("group", "sample"), None),
        ),
        check_vma=False,
    )
```

```python
import math

import jax
import jax.numpy as jnp
from jax import lax
from jax.experimental import pallas as pl
from jax.experimental.pallas import tpu as pltpu
from jax.sharding import PartitionSpec as P

NEG_FILL = -1e30
HEADS_PER_STEP = 8
LAT = 512
WIDE = 640
BF = jnp.bfloat16
F32 = jnp.float32


def spread_weights(w_key, w_value, copies):
    rows, cols = w_key.shape

    def kernel(key_ref, value_ref, out_ref, sems):
        moves = []
        for j in range(copies):
            moves.append(pltpu.make_async_copy(key_ref, out_ref.at[j, pl.ds(0, rows)], sems.at[2 * j]))
            moves.append(pltpu.make_async_copy(value_ref, out_ref.at[j, pl.ds(rows, rows)], sems.at[2 * j + 1]))
        for move in moves:
            move.start()
        for move in moves:
            move.wait()

    return pl.pallas_call(
        kernel,
        out_shape=pltpu.HBM((copies, 2 * rows, cols), BF),
        in_specs=[pl.BlockSpec(memory_space=pltpu.VMEM)] * 2,
        out_specs=pl.BlockSpec(memory_space=pl.ANY),
        scratch_shapes=[pltpu.SemaphoreType.DMA((2 * copies,))],
        compiler_params=pltpu.CompilerParams(vmem_limit_bytes=2 * 2**20),
        name="spread_weights",
    )(w_key, w_value)


def turn3(number):
    low = lax.shift_left(jnp.bitwise_and(number, 1), 2)
    return low + jnp.bitwise_and(number, 2) + lax.shift_right_logical(number, 2)


def dot(left, right, dims):
    return lax.dot_general(left, right, (dims, ((), ())), preferred_element_type=F32)


def attention(facts, q_nope, q_rope, out_grad, keys, w_own, w_other):
    row_count = q_nope.shape[0]
    key_count = keys.shape[0]
    prompt_count = key_count - row_count
    head_count = q_nope.shape[1] // 128
    hps = HEADS_PER_STEP
    steps = head_count // hps
    chips, two_rows, _ = w_own.shape
    w_rows = two_rows // 2
    ctx_count = 8
    owned = prompt_count // ctx_count
    resp_owned = row_count // ctx_count
    scale = 1.0 / math.sqrt(192.0)
    exp_scale = scale * math.log2(math.e)

    def kernel(facts_ref, qn_ref, qr_ref, og_ref, keys_ref, wk_own, wv_own, wk_oth, wv_oth,
               out_ref, gqn_ref, gqr_ref, prompt_ref, resp_ref, w_all, bias, live, acc, acc_rope):
        step = pl.program_id(0)
        length, offset, ctx, core = facts_ref[0], facts_ref[1], facts_ref[2], facts_ref[3]

        @pl.when(step == 0)
        def _():
            key = lax.broadcasted_iota(jnp.int32, (key_count, row_count), 0)
            slot = lax.broadcasted_iota(jnp.int32, (key_count, row_count), 1)
            block = lax.shift_right_logical(key, 5)
            place = jnp.bitwise_xor(turn3(block), ctx) * owned + jnp.bitwise_and(key, owned - 1)
            bias[...] = jnp.where(
                key < prompt_count,
                jnp.where(place < offset, 0.0, NEG_FILL),
                jnp.where(key - prompt_count <= slot, 0.0, NEG_FILL))
            row = lax.broadcasted_iota(jnp.int32, (row_count, 128), 0)
            live[...] = jnp.where(row < length, 1.0, 0.0)
            acc[...] = jnp.zeros_like(acc)
            acc_rope[...] = jnp.zeros_like(acc_rope)

        for j in range(chips):
            own_at = pl.ds(pl.multiple_of(j * 2 * w_rows + core * w_rows, w_rows), w_rows)
            oth_at = pl.ds(pl.multiple_of(j * 2 * w_rows + (1 - core) * w_rows, w_rows), w_rows)
            for h in range(hps):
                src = slice(128 * h, 128 * h + 128)
                w_all[own_at, 256 * h:256 * h + 128] = wk_own[j, :, src]
                w_all[own_at, 256 * h + 128:256 * h + 256] = wv_own[j, :, src]
                w_all[oth_at, 256 * h:256 * h + 128] = wk_oth[j, :, src]
                w_all[oth_at, 256 * h + 128:256 * h + 256] = wv_oth[j, :, src]

        keys_lat = keys_ref[:, :LAT]
        keys_rot = keys_ref[:, LAT:]
        alive = live[...]
        lane = lax.broadcasted_iota(jnp.int32, (row_count, 128), 1)
        heads = range(hps)
        cols = [slice(128 * h, 128 * h + 128) for h in heads]
        both = [dot(keys_lat, w_all[:, 256 * h:256 * h + 256], ((1,), (0,))).astype(BF) for h in heads]
        value = [b[:, 128:] for b in both]
        key_full = [jnp.concatenate([b[:, :128], keys_rot], axis=1) for b in both]
        query = []
        for h in heads:
            mine = (lane < 64) if h % 2 == 0 else (lane >= 64)
            rope = jnp.where(mine, qr_ref[:, 128 * (h // 2):128 * (h // 2) + 128].astype(F32), 0.0).astype(BF)
            query.append(jnp.concatenate([qn_ref[:, cols[h]], rope], axis=1))
        grad_out = [(og_ref[:, c].astype(F32) * alive).astype(BF) for c in cols]
        scores = [dot(key_full[h], query[h], ((1,), (1,))) + bias[...] for h in heads]
        grad_prob = [dot(value[h], grad_out[h], ((1,), (1,))) for h in heads]
        prob_half, grad_score = [], []
        for h in heads:
            top = jnp.max(scores[h], axis=0, keepdims=True)
            raised = jnp.exp2((scores[h] - top) * exp_scale)
            prob = raised * (1.0 / jnp.sum(raised, axis=0, keepdims=True))
            prob_half.append(prob.astype(BF))
            weighed = prob * grad_prob[h]
            inner = jnp.sum(weighed, axis=0, keepdims=True)
            grad_score.append(((weighed - prob * inner) * scale).astype(BF))
        attn = [dot(prob_half[h], value[h], ((0,), (0,))) for h in heads]
        grad_query = [dot(grad_score[h], key_full[h], ((0,), (0,))) for h in heads]
        grad_key = [dot(grad_score[h], query[h], ((1,), (0,))) for h in heads]
        grad_value = [dot(prob_half[h], grad_out[h], ((1,), (0,))) for h in heads]
        grads = []
        rope_sum = None
        for h in heads:
            out_ref[:, cols[h]] = (attn[h] * alive).astype(BF)
            gqn_ref[:, cols[h]] = grad_query[h][:, :128].astype(BF)
            if h % 2 == 1:
                gqr_ref[:, cols[h // 2]] = jnp.where(
                    lane < 64, grad_query[h - 1][:, 128:], grad_query[h][:, 128:]).astype(BF)
            grads += [grad_key[h][:, :128].astype(BF), grad_value[h].astype(BF)]
            rope_sum = grad_key[h][:, 128:] if rope_sum is None else rope_sum + grad_key[h][:, 128:]
        acc[...] += dot(jnp.concatenate(grads, axis=1), w_all[...], ((1,), (1,)))
        acc_rope[...] += rope_sum

        @pl.when(step == steps - 1)
        def _():
            for owner in range(ctx_count):
                at = pl.ds(pl.multiple_of(turn3(jnp.bitwise_xor(ctx, owner)) * owned, owned), owned)
                prompt_ref[owner, :, :LAT] = acc[at, :].astype(BF)
                prompt_ref[owner, :, LAT:] = acc_rope[at, :].astype(BF)
                at = slice(prompt_count + owner * resp_owned, prompt_count + (owner + 1) * resp_owned)
                resp_ref[owner, :, :LAT] = acc[at, :].astype(BF)
                resp_ref[owner, :, LAT:] = acc_rope[at, :].astype(BF)

    wide = 128 * hps
    return pl.pallas_call(
        kernel,
        grid=(steps,),
        in_specs=[
            pl.BlockSpec(memory_space=pltpu.SMEM),
            pl.BlockSpec((row_count, wide), lambda i: (0, i)),
            pl.BlockSpec((row_count, wide // 2), lambda i: (0, i)),
            pl.BlockSpec((row_count, wide), lambda i: (0, i)),
            pl.BlockSpec((key_count, WIDE), lambda i: (0, 0)),
            pl.BlockSpec((chips, w_rows, wide), lambda i: (0, 0, i)),
            pl.BlockSpec((chips, w_rows, wide), lambda i: (0, 1, i)),
            pl.BlockSpec((chips, w_rows, wide), lambda i: (0, 0, i)),
            pl.BlockSpec((chips, w_rows, wide), lambda i: (0, 1, i)),
        ],
        out_specs=[
            pl.BlockSpec((row_count, wide), lambda i: (0, i)),
            pl.BlockSpec((row_count, wide), lambda i: (0, i)),
            pl.BlockSpec((row_count, wide // 2), lambda i: (0, i)),
            pl.BlockSpec((ctx_count, owned, WIDE), lambda i: (0, 0, 0)),
            pl.BlockSpec((ctx_count, resp_owned, WIDE), lambda i: (0, 0, 0)),
        ],
        out_shape=[
            jax.ShapeDtypeStruct(q_nope.shape, BF),
            jax.ShapeDtypeStruct(q_nope.shape, BF),
            jax.ShapeDtypeStruct(q_rope.shape, BF),
            pltpu.HBM((ctx_count, owned, WIDE), BF),
            pltpu.HBM((ctx_count, resp_owned, WIDE), BF),
        ],
        scratch_shapes=[
            pltpu.VMEM((LAT, 256 * hps), BF),
            pltpu.VMEM((key_count, row_count), F32),
            pltpu.VMEM((row_count, 128), F32),
            pltpu.VMEM((key_count, LAT), F32),
            pltpu.VMEM((key_count, 128), F32),
        ],
        compiler_params=pltpu.CompilerParams(vmem_limit_bytes=28 * 2**20),
        cost_estimate=pl.CostEstimate(flops=6 * 10**9, bytes_accessed=8 * 2**20, transcendentals=2048 * 384),
        name="attention",
    )(facts, q_nope, q_rope, out_grad, keys, w_own, w_own, w_other, w_other)


def add_resp(terms, prompt_terms):
    def kernel(terms_ref, through_ref, resp_ref, out_ref):
        del through_ref, out_ref
        total = terms_ref[0].astype(F32)
        for j in range(1, terms.shape[0]):
            total = total + terms_ref[j].astype(F32)
        resp_ref[...] = total.astype(BF)

    return pl.pallas_call(
        kernel,
        in_specs=[pl.BlockSpec(memory_space=pltpu.VMEM), pl.BlockSpec(memory_space=pl.ANY)],
        out_specs=[pl.BlockSpec(memory_space=pltpu.VMEM), pl.BlockSpec(memory_space=pl.ANY)],
        out_shape=[
            jax.ShapeDtypeStruct(terms.shape[1:], BF),
            pltpu.HBM(prompt_terms.shape, BF),
        ],
        input_output_aliases={1: 1},
        compiler_params=pltpu.CompilerParams(vmem_limit_bytes=4 * 2**20),
        name="add_resp",
    )(terms, prompt_terms)


def add_prompt(terms, copies):
    owned = terms.shape[1]

    def kernel(terms_ref, prompt_ref, held, sems):
        total = terms_ref[0].astype(F32)
        for j in range(1, terms.shape[0]):
            total = total + terms_ref[j].astype(F32)
        held[...] = total.astype(BF)
        moves = [pltpu.make_async_copy(held, prompt_ref.at[j], sems.at[j]) for j in range(copies)]
        for move in moves:
            move.start()
        for move in moves:
            move.wait()

    return pl.pallas_call(
        kernel,
        in_specs=[pl.BlockSpec(memory_space=pltpu.VMEM)],
        out_specs=pl.BlockSpec(memory_space=pl.ANY),
        out_shape=pltpu.HBM((copies, owned, WIDE), BF),
        scratch_shapes=[pltpu.VMEM((owned, WIDE), BF), pltpu.SemaphoreType.DMA((copies,))],
        compiler_params=pltpu.CompilerParams(vmem_limit_bytes=4 * 2**20),
        name="add_prompt",
    )(terms)


def finish(facts, prompt_terms, resp_sum):
    samples, owned, _ = prompt_terms.shape
    row_count = resp_sum.shape[0]
    resp_owned = row_count // 8

    def kernel(facts_ref, prompt_ref, resp_ref, plat_ref, prot_ref, rlat_ref, rrot_ref, held):
        ctx = facts_ref[2]
        total = prompt_ref[0].astype(F32)
        for j in range(1, samples):
            total = total + prompt_ref[j].astype(F32)
        plat_ref[...] = total[:, :LAT]
        prot_ref[...] = total[:, LAT:LAT + 64] + total[:, LAT + 64:]
        for owner in range(8):
            at = pl.ds(pl.multiple_of(turn3(jnp.bitwise_xor(ctx, owner)) * resp_owned, resp_owned), resp_owned)
            rows = resp_ref[at, :].astype(F32)
            to = slice(owner * resp_owned, (owner + 1) * resp_owned)
            rlat_ref[to, :] = rows[:, :LAT]
            held[to, :] = rows[:, LAT:]
        turned = jnp.swapaxes(held[...], 0, 1)
        rrot_ref[...] = turned[:64] + turned[64:]

    vm = pl.BlockSpec(memory_space=pltpu.VMEM)
    return pl.pallas_call(
        kernel,
        in_specs=[pl.BlockSpec(memory_space=pltpu.SMEM), vm, vm],
        out_specs=[vm] * 4,
        out_shape=[
            jax.ShapeDtypeStruct((owned, LAT), F32),
            jax.ShapeDtypeStruct((owned, 64), F32),
            jax.ShapeDtypeStruct((row_count, LAT), F32),
            jax.ShapeDtypeStruct((64, row_count), F32),
        ],
        scratch_shapes=[pltpu.VMEM((row_count, 128), F32)],
        compiler_params=pltpu.CompilerParams(vmem_limit_bytes=4 * 2**20),
        name="finish",
    )(facts, prompt_terms, resp_sum)


def butterfly(block, distances=(4, 2, 1)):
    for k in distances:
        block = jnp.concatenate([block, lax.ppermute(block, "ctx", [(i, i ^ k) for i in range(8)])], axis=0)
    return block


def per_device(
    q_nope,
    q_rope,
    prompt_latent,
    prompt_rope,
    resp_latent,
    resp_rope,
    w_key,
    w_value,
    out_grad,
    lengths,
    offsets,
):
    ctx = lax.axis_index("ctx").astype(jnp.int32)
    core = jnp.bitwise_and(lax.axis_index("sample").astype(jnp.int32), 1)
    facts = jnp.concatenate([lengths, offsets, ctx[None], core[None]])
    same_core = [[2 * chip + c for chip in range(8)] for c in range(2)]
    w_own = lax.all_to_all(
        spread_weights(w_key, w_value, 8), "sample", 0, 0, tiled=True, axis_index_groups=same_core)
    prompt_keys = butterfly(jnp.concatenate([prompt_latent, prompt_rope, prompt_rope], axis=1))
    keys = jnp.concatenate(
        [prompt_keys, jnp.concatenate([resp_latent, resp_rope, resp_rope], axis=1)], axis=0)
    w_own, keys = lax.optimization_barrier((w_own, keys))
    w_other = lax.ppermute(w_own, "sample", [(i, i ^ 1) for i in range(16)])
    attn_out, grad_query_nope, grad_query_rope, prompt_terms, resp_terms = attention(
        facts, q_nope, q_rope, out_grad, keys, w_own, w_other)
    resp_terms = lax.all_to_all(resp_terms, "ctx", 0, 0, tiled=True)
    resp_part, prompt_terms = add_resp(resp_terms, prompt_terms)
    prompt_terms = lax.all_to_all(prompt_terms, "ctx", 0, 0, tiled=True)
    resp_half, prompt_terms = lax.optimization_barrier((butterfly(resp_part, (4,)), prompt_terms))
    resp_sum = butterfly(resp_half, (2, 1))
    prompt_part = lax.all_to_all(add_prompt(prompt_terms, 16), "sample", 0, 0, tiled=True)
    prompt_lat, prompt_rot, resp_lat, resp_rot = finish(facts, prompt_part, resp_sum)
    return (attn_out, grad_query_nope, grad_query_rope, prompt_lat, prompt_rot, resp_lat, resp_rot.T)


def solution(mesh):
    placed = (
        P(("group", "sample"), "ctx"),
        P(("group", "sample"), "ctx"),
        P(("group", "ctx"), None),
        P(("group", "ctx"), None),
        P(("group", "sample"), None),
        P(("group", "sample"), None),
        P("sample", "ctx"),
        P("sample", "ctx"),
        P(("group", "sample"), "ctx"),
        P(("group", "sample")),
        P(("group", "sample")),
    )
    return jax.shard_map(
        per_device,
        mesh=mesh,
        in_specs=placed,
        out_specs=(
            P(("group", "sample"), "ctx"),
            P(("group", "sample"), "ctx"),
            P(("group", "sample"), "ctx"),
            P(("group", "ctx"), None),
            P(("group", "ctx"), None),
            P(("group", "sample"), None),
            P(("group", "sample"), None),
        ),
        check_vma=False,
    )
```

```python
import math

import jax
import jax.numpy as jnp
from jax import lax
from jax.experimental import pallas as pl
from jax.experimental.pallas import tpu as pltpu
from jax.sharding import PartitionSpec as P

NEG_FILL = -1e30
HEADS_PER_STEP = 8
LAT = 512
WIDE = 640
BF = jnp.bfloat16
F32 = jnp.float32


def spread_weights(w_key, w_value, copies):
    rows, cols = w_key.shape

    def kernel(key_ref, value_ref, out_ref, held, sems):
        moves = [
            pltpu.make_async_copy(key_ref, held.at[pl.ds(0, rows)], sems.at[0]),
            pltpu.make_async_copy(value_ref, held.at[pl.ds(rows, rows)], sems.at[1]),
        ]
        for move in moves:
            move.start()
        for move in moves:
            move.wait()
        moves = [pltpu.make_async_copy(held, out_ref.at[j], sems.at[j]) for j in range(copies)]
        for move in moves:
            move.start()
        for move in moves:
            move.wait()

    return pl.pallas_call(
        kernel,
        out_shape=pltpu.HBM((copies, 2 * rows, cols), BF),
        in_specs=[pl.BlockSpec(memory_space=pltpu.HBM)] * 2,
        out_specs=pl.BlockSpec(memory_space=pl.ANY),
        scratch_shapes=[pltpu.VMEM((2 * rows, cols), BF), pltpu.SemaphoreType.DMA((copies,))],
        compiler_params=pltpu.CompilerParams(vmem_limit_bytes=58 * 2**20),
        name="spread_weights",
    )(w_key, w_value)


def block_of(distance):
    return 2 * jnp.bitwise_and(distance, 3) + lax.shift_right_logical(distance, 2)


def dot(left, right, dims):
    return lax.dot_general(left, right, (dims, ((), ())), preferred_element_type=F32)


def join_keys(pieces, resp_latent, resp_rope):
    piece_rows = pieces[0].shape[0]
    prompt_count = piece_rows * len(pieces)
    key_count = prompt_count + resp_latent.shape[0]

    def kernel(piece_0, piece_1, piece_2, piece_3, lat_ref, rot_ref, keys_ref):
        for j, piece in enumerate((piece_0, piece_1, piece_2, piece_3)):
            keys_ref[j * piece_rows:(j + 1) * piece_rows] = piece[...]
        keys_ref[prompt_count:, :LAT] = lat_ref[...]
        turned = rot_ref[...].astype(F32)
        turned = jnp.concatenate([turned, turned], axis=0)
        keys_ref[prompt_count:, LAT:] = jnp.swapaxes(turned, 0, 1).astype(BF)

    return pl.pallas_call(
        kernel,
        in_specs=[pl.BlockSpec(memory_space=pltpu.VMEM)] * 6,
        out_specs=pl.BlockSpec(memory_space=pltpu.VMEM),
        out_shape=jax.ShapeDtypeStruct((key_count, WIDE), BF),
        compiler_params=pltpu.CompilerParams(vmem_limit_bytes=4 * 2**20),
        name="join_keys",
    )(*pieces, resp_latent, resp_rope.T)


def attention(facts, q_nope, q_rope, out_grad, keys, w_own, w_other):
    row_count = q_nope.shape[0]
    key_count = keys.shape[0]
    prompt_count = key_count - row_count
    head_count = q_nope.shape[1] // 128
    hps = HEADS_PER_STEP
    steps = head_count // hps
    chips, two_rows, _ = w_own.shape
    w_rows = two_rows // 2
    ctx_count = 8
    owned = prompt_count // ctx_count
    resp_owned = row_count // 4
    scale = 1.0 / math.sqrt(192.0)
    exp_scale = scale * math.log2(math.e)

    def kernel(facts_ref, qn_ref, qr_ref, og_ref, keys_ref, wk_own, wv_own, wk_oth, wv_oth,
               out_ref, gqn_ref, gqr_ref, terms_ref,
               w_all, bias, live, acc, acc_rope):
        step = pl.program_id(0)
        length, offset, ctx, core = facts_ref[0], facts_ref[1], facts_ref[2], facts_ref[3]

        @pl.when(step == 0)
        def _():
            key = lax.broadcasted_iota(jnp.int32, (key_count, row_count), 0)
            slot = lax.broadcasted_iota(jnp.int32, (key_count, row_count), 1)
            block = lax.shift_right_logical(key, 5)
            distance = lax.shift_right_logical(block, 1) + 4 * jnp.bitwise_and(block, 1)
            place = jnp.bitwise_xor(distance, ctx) * owned + jnp.bitwise_and(key, owned - 1)
            bias[...] = jnp.where(
                key < prompt_count,
                jnp.where(place < offset, 0.0, NEG_FILL),
                jnp.where(key - prompt_count <= slot, 0.0, NEG_FILL))
            row = lax.broadcasted_iota(jnp.int32, (row_count, 128), 0)
            live[...] = jnp.where(row < length, 1.0, 0.0)
            acc[...] = jnp.zeros_like(acc)
            acc_rope[...] = jnp.zeros_like(acc_rope)

        for j in range(chips):
            own_at = pl.ds(pl.multiple_of(j * 2 * w_rows + core * w_rows, w_rows), w_rows)
            oth_at = pl.ds(pl.multiple_of(j * 2 * w_rows + (1 - core) * w_rows, w_rows), w_rows)
            for h in range(hps):
                src = slice(128 * h, 128 * h + 128)
                w_all[own_at, 256 * h:256 * h + 128] = wk_own[j, :, src]
                w_all[own_at, 256 * h + 128:256 * h + 256] = wv_own[j, :, src]
                w_all[oth_at, 256 * h:256 * h + 128] = wk_oth[j, :, src]
                w_all[oth_at, 256 * h + 128:256 * h + 256] = wv_oth[j, :, src]

        keys_lat = keys_ref[:, :LAT]
        keys_rot = keys_ref[:, LAT:]
        alive = live[...]
        lane = lax.broadcasted_iota(jnp.int32, (row_count, 128), 1)
        heads = range(hps)
        cols = [slice(128 * h, 128 * h + 128) for h in heads]
        both = [dot(keys_lat, w_all[:, 256 * h:256 * h + 256], ((1,), (0,))).astype(BF) for h in heads]
        value = [b[:, 128:] for b in both]
        key_full = [jnp.concatenate([b[:, :128], keys_rot], axis=1) for b in both]
        query = []
        for h in heads:
            mine = (lane < 64) if h % 2 == 0 else (lane >= 64)
            rope = jnp.where(mine, qr_ref[:, 128 * (h // 2):128 * (h // 2) + 128].astype(F32), 0.0).astype(BF)
            query.append(jnp.concatenate([qn_ref[:, cols[h]], rope], axis=1))
        grad_out = [(og_ref[:, c].astype(F32) * alive).astype(BF) for c in cols]
        scores = [dot(key_full[h], query[h], ((1,), (1,))) + bias[...] for h in heads]
        grad_prob = [dot(value[h], grad_out[h], ((1,), (1,))) for h in heads]
        prob_half, grad_score = [], []
        for h in heads:
            top = jnp.max(scores[h], axis=0, keepdims=True)
            raised = jnp.exp2((scores[h] - top) * exp_scale)
            prob = raised * (1.0 / jnp.sum(raised, axis=0, keepdims=True))
            prob_half.append(prob.astype(BF))
            weighed = prob * grad_prob[h]
            inner = jnp.sum(weighed, axis=0, keepdims=True)
            grad_score.append(((weighed - prob * inner) * scale).astype(BF))
        attn = [dot(prob_half[h], value[h], ((0,), (0,))) for h in heads]
        grad_query = [dot(grad_score[h], key_full[h], ((0,), (0,))) for h in heads]
        grad_key = [dot(grad_score[h], query[h], ((1,), (0,))) for h in heads]
        grad_value = [dot(prob_half[h], grad_out[h], ((1,), (0,))) for h in heads]
        grads = []
        rope_sum = None
        for h in heads:
            out_ref[:, cols[h]] = (attn[h] * alive).astype(BF)
            gqn_ref[:, cols[h]] = grad_query[h][:, :128].astype(BF)
            if h % 2 == 1:
                gqr_ref[:, cols[h // 2]] = jnp.where(
                    lane < 64, grad_query[h - 1][:, 128:], grad_query[h][:, 128:]).astype(BF)
            grads += [grad_key[h][:, :128].astype(BF), grad_value[h].astype(BF)]
            rope_sum = grad_key[h][:, 128:] if rope_sum is None else rope_sum + grad_key[h][:, 128:]
        acc[...] += dot(jnp.concatenate(grads, axis=1), w_all[...], ((1,), (1,)))
        acc_rope[...] += rope_sum

        @pl.when(step == steps - 1)
        def _():
            for owner in range(ctx_count):
                at = pl.ds(pl.multiple_of(block_of(jnp.bitwise_xor(ctx, owner)) * owned, owned), owned)
                terms_ref[owner, :owned, :LAT] = acc[at, :].astype(BF)
                terms_ref[owner, :owned, LAT:] = acc_rope[at, :].astype(BF)
                first = prompt_count + (owner % 4) * resp_owned
                at = slice(first, first + resp_owned)
                terms_ref[owner, owned:, :LAT] = acc[at, :].astype(BF)
                terms_ref[owner, owned:, LAT:] = acc_rope[at, :].astype(BF)

    wide = 128 * hps
    return pl.pallas_call(
        kernel,
        grid=(steps,),
        in_specs=[
            pl.BlockSpec(memory_space=pltpu.SMEM),
            pl.BlockSpec((row_count, wide), lambda i: (0, i)),
            pl.BlockSpec((row_count, wide // 2), lambda i: (0, i)),
            pl.BlockSpec((row_count, wide), lambda i: (0, i)),
            pl.BlockSpec((key_count, WIDE), lambda i: (0, 0)),
            pl.BlockSpec((chips, w_rows, wide), lambda i: (0, 0, i)),
            pl.BlockSpec((chips, w_rows, wide), lambda i: (0, 1, i)),
            pl.BlockSpec((chips, w_rows, wide), lambda i: (0, 0, i)),
            pl.BlockSpec((chips, w_rows, wide), lambda i: (0, 1, i)),
        ],
        out_specs=[
            pl.BlockSpec((row_count, wide), lambda i: (0, i)),
            pl.BlockSpec((row_count, wide), lambda i: (0, i)),
            pl.BlockSpec((row_count, wide // 2), lambda i: (0, i)),
            pl.BlockSpec((ctx_count, owned + resp_owned, WIDE), lambda i: (0, 0, 0)),
        ],
        out_shape=[
            jax.ShapeDtypeStruct(q_nope.shape, BF),
            jax.ShapeDtypeStruct(q_nope.shape, BF),
            jax.ShapeDtypeStruct(q_rope.shape, BF),
            pltpu.HBM((ctx_count, owned + resp_owned, WIDE), BF),
        ],
        scratch_shapes=[
            pltpu.VMEM((LAT, 256 * hps), BF),
            pltpu.VMEM((key_count, row_count), F32),
            pltpu.VMEM((row_count, 128), F32),
            pltpu.VMEM((key_count, LAT), F32),
            pltpu.VMEM((key_count, 128), F32),
        ],
        compiler_params=pltpu.CompilerParams(vmem_limit_bytes=28 * 2**20),
        cost_estimate=pl.CostEstimate(flops=6 * 10**9, bytes_accessed=8 * 2**20, transcendentals=2048 * 384),
        name="attention",
    )(facts, q_nope, q_rope, out_grad, keys, w_own, w_own, w_other, w_other)


def add_heads(terms, owned, copies):
    resp_owned = terms.shape[1] - owned

    def kernel(terms_ref, prompt_ref, resp_ref, held, sems):
        def total(at):
            result = terms_ref[0, at].astype(F32)
            for j in range(1, terms.shape[0]):
                result = result + terms_ref[j, at].astype(F32)
            return result.astype(BF)

        held[...] = total(slice(0, owned))
        moves = [pltpu.make_async_copy(held, prompt_ref.at[j], sems.at[j]) for j in range(copies)]
        for move in moves:
            move.start()
        resp_ref[...] = total(slice(owned, owned + resp_owned))
        for move in moves:
            move.wait()

    return pl.pallas_call(
        kernel,
        in_specs=[pl.BlockSpec(memory_space=pltpu.VMEM)],
        out_specs=[pl.BlockSpec(memory_space=pl.ANY), pl.BlockSpec(memory_space=pltpu.VMEM)],
        out_shape=[
            pltpu.HBM((copies, owned, WIDE), BF),
            jax.ShapeDtypeStruct((resp_owned, WIDE), BF),
        ],
        scratch_shapes=[pltpu.VMEM((owned, WIDE), BF), pltpu.SemaphoreType.DMA((copies,))],
        compiler_params=pltpu.CompilerParams(vmem_limit_bytes=4 * 2**20),
        name="add_heads",
    )(terms)


def finish(facts, prompt_terms, resp_pieces):
    samples, owned, _ = prompt_terms.shape
    piece_rows = resp_pieces[0].shape[0]
    row_count = piece_rows * len(resp_pieces)
    def kernel(facts_ref, prompt_ref, piece_0, piece_1, piece_2, piece_3, plat_ref, prot_ref, rlat_ref, rrot_ref, held):
        ctx = facts_ref[2]
        total = prompt_ref[0].astype(F32)
        for j in range(1, samples):
            total = total + prompt_ref[j].astype(F32)
        plat_ref[...] = total[:, :LAT]
        prot_ref[...] = total[:, LAT:LAT + 64] + total[:, LAT + 64:]
        for distance, piece in enumerate((piece_0, piece_1, piece_2, piece_3)):
            start = jnp.bitwise_xor(jnp.bitwise_and(ctx, 3), distance) * piece_rows
            at = pl.ds(pl.multiple_of(start, piece_rows), piece_rows)
            rows = piece[...].astype(F32)
            rlat_ref[at, :] = rows[:, :LAT]
            held[at, :] = rows[:, LAT:]
        turned = jnp.swapaxes(held[...], 0, 1)
        rrot_ref[...] = turned[:64] + turned[64:]

    vm = pl.BlockSpec(memory_space=pltpu.VMEM)
    return pl.pallas_call(
        kernel,
        in_specs=[pl.BlockSpec(memory_space=pltpu.SMEM)] + [vm] * 5,
        out_specs=[vm] * 4,
        out_shape=[
            jax.ShapeDtypeStruct((owned, LAT), F32),
            jax.ShapeDtypeStruct((owned, 64), F32),
            jax.ShapeDtypeStruct((row_count, LAT), F32),
            jax.ShapeDtypeStruct((64, row_count), F32),
        ],
        scratch_shapes=[pltpu.VMEM((row_count, 128), F32)],
        compiler_params=pltpu.CompilerParams(vmem_limit_bytes=4 * 2**20),
        name="finish",
    )(facts, prompt_terms, *resp_pieces)


def from_distance(block, distance):
    return lax.ppermute(block, "ctx", [(i, i ^ distance) for i in range(8)])


def meet(block):
    return jnp.concatenate([block, from_distance(block, 4)], axis=0)


def share(block):
    return [block] + [from_distance(block, distance) for distance in (3, 2, 1)][::-1]


def per_device(
    q_nope,
    q_rope,
    prompt_latent,
    prompt_rope,
    resp_latent,
    resp_rope,
    w_key,
    w_value,
    out_grad,
    lengths,
    offsets,
):
    ctx = lax.axis_index("ctx").astype(jnp.int32)
    core = jnp.bitwise_and(lax.axis_index("sample").astype(jnp.int32), 1)
    facts = jnp.concatenate([lengths, offsets, ctx[None], core[None]])
    same_core = [[2 * chip + c for chip in range(8)] for c in range(2)]
    w_own = lax.all_to_all(
        spread_weights(w_key, w_value, 8), "sample", 0, 0, tiled=True, axis_index_groups=same_core)
    prompt_pieces = share(meet(jnp.concatenate([prompt_latent, prompt_rope, prompt_rope], axis=1)))
    keys = join_keys(prompt_pieces, resp_latent, resp_rope)
    w_own, keys = lax.optimization_barrier((w_own, keys))
    w_other = lax.ppermute(w_own, "sample", [(i, i ^ 1) for i in range(16)])
    attn_out, grad_query_nope, grad_query_rope, terms = attention(
        facts, q_nope, q_rope, out_grad, keys, w_own, w_other)
    terms = lax.all_to_all(terms, "ctx", 0, 0, tiled=True)
    prompt_part, resp_part = add_heads(terms, prompt_latent.shape[0], 16)
    prompt_part = lax.all_to_all(prompt_part, "sample", 0, 0, tiled=True)
    resp_pieces = share(resp_part)
    prompt_lat, prompt_rot, resp_lat, resp_rot = finish(facts, prompt_part, resp_pieces)
    return (attn_out, grad_query_nope, grad_query_rope, prompt_lat, prompt_rot, resp_lat, resp_rot.T)


def solution(mesh):
    placed = (
        P(("group", "sample"), "ctx"),
        P(("group", "sample"), "ctx"),
        P(("group", "ctx"), None),
        P(("group", "ctx"), None),
        P(("group", "sample"), None),
        P(("group", "sample"), None),
        P("sample", "ctx"),
        P("sample", "ctx"),
        P(("group", "sample"), "ctx"),
        P(("group", "sample")),
        P(("group", "sample")),
    )
    return jax.shard_map(
        per_device,
        mesh=mesh,
        in_specs=placed,
        out_specs=(
            P(("group", "sample"), "ctx"),
            P(("group", "sample"), "ctx"),
            P(("group", "sample"), "ctx"),
            P(("group", "ctx"), None),
            P(("group", "ctx"), None),
            P(("group", "sample"), None),
            P(("group", "sample"), None),
        ),
        check_vma=False,
    )
```

```python
import math

import jax
import jax.numpy as jnp
from jax import lax
from jax.experimental import pallas as pl
from jax.experimental.pallas import tpu as pltpu
from jax.sharding import PartitionSpec as P

NEG_FILL = -1e30
HEADS_PER_STEP = 8
LAT = 512
WIDE = 640
BF = jnp.bfloat16
F32 = jnp.float32


def spread_weights(w_key, w_value, copies):
    rows, cols = w_key.shape

    def kernel(key_ref, value_ref, out_ref, held, sems):
        moves = [
            pltpu.make_async_copy(key_ref, held.at[pl.ds(0, rows)], sems.at[0]),
            pltpu.make_async_copy(value_ref, held.at[pl.ds(rows, rows)], sems.at[1]),
        ]
        for move in moves:
            move.start()
        for move in moves:
            move.wait()
        moves = [pltpu.make_async_copy(held, out_ref.at[j], sems.at[j]) for j in range(copies)]
        for move in moves:
            move.start()
        for move in moves:
            move.wait()

    return pl.pallas_call(
        kernel,
        out_shape=pltpu.HBM((copies, 2 * rows, cols), BF),
        in_specs=[pl.BlockSpec(memory_space=pltpu.HBM)] * 2,
        out_specs=pl.BlockSpec(memory_space=pl.ANY),
        scratch_shapes=[pltpu.VMEM((2 * rows, cols), BF), pltpu.SemaphoreType.DMA((copies,))],
        compiler_params=pltpu.CompilerParams(vmem_limit_bytes=58 * 2**20),
        name="spread_weights",
    )(w_key, w_value)


def block_of(distance):
    return 2 * jnp.bitwise_and(distance, 3) + lax.shift_right_logical(distance, 2)


def dot(left, right, dims):
    return lax.dot_general(left, right, (dims, ((), ())), preferred_element_type=F32)


def join_keys(pieces, resp_latent, resp_rope):
    piece_rows = pieces[0].shape[0]
    prompt_count = piece_rows * len(pieces)
    key_count = prompt_count + resp_latent.shape[0]

    def kernel(piece_0, piece_1, piece_2, piece_3, lat_ref, rot_ref, keys_ref):
        for j, piece in enumerate((piece_0, piece_1, piece_2, piece_3)):
            keys_ref[j * piece_rows:(j + 1) * piece_rows] = piece[...]
        keys_ref[prompt_count:, :LAT] = lat_ref[...]
        turned = rot_ref[...].astype(F32)
        turned = jnp.concatenate([turned, turned], axis=0)
        keys_ref[prompt_count:, LAT:] = jnp.swapaxes(turned, 0, 1).astype(BF)

    return pl.pallas_call(
        kernel,
        in_specs=[pl.BlockSpec(memory_space=pltpu.VMEM)] * 6,
        out_specs=pl.BlockSpec(memory_space=pltpu.VMEM),
        out_shape=jax.ShapeDtypeStruct((key_count, WIDE), BF),
        compiler_params=pltpu.CompilerParams(vmem_limit_bytes=4 * 2**20),
        name="join_keys",
    )(*pieces, resp_latent, resp_rope.T)


def attention(for_keys, facts, q_nope, q_rope, out_grad, keys, w_own, w_other):
    row_count = q_nope.shape[0]
    key_count = keys.shape[0]
    prompt_count = key_count - row_count
    head_count = q_nope.shape[1] // 128
    hps = HEADS_PER_STEP
    steps = head_count // hps
    chips, two_rows, _ = w_own.shape
    w_rows = two_rows // 2
    ctx_count = 8
    owned = prompt_count // ctx_count
    resp_owned = row_count // 4
    scale = 1.0 / math.sqrt(192.0)
    exp_scale = scale * math.log2(math.e)

    def kernel(facts_ref, qn_ref, qr_ref, og_ref, keys_ref, wk_own, wv_own, wk_oth, wv_oth, *refs):
        if for_keys:
            terms_ref, w_all, bias, live, acc, acc_rope = refs
        else:
            out_ref, gqn_ref, gqr_ref, w_all, bias, live = refs
        step = pl.program_id(0)
        length, offset, ctx, core = facts_ref[0], facts_ref[1], facts_ref[2], facts_ref[3]

        @pl.when(step == 0)
        def _():
            key = lax.broadcasted_iota(jnp.int32, (key_count, row_count), 0)
            slot = lax.broadcasted_iota(jnp.int32, (key_count, row_count), 1)
            block = lax.shift_right_logical(key, 5)
            distance = lax.shift_right_logical(block, 1) + 4 * jnp.bitwise_and(block, 1)
            place = jnp.bitwise_xor(distance, ctx) * owned + jnp.bitwise_and(key, owned - 1)
            bias[...] = jnp.where(
                key < prompt_count,
                jnp.where(place < offset, 0.0, NEG_FILL),
                jnp.where(key - prompt_count <= slot, 0.0, NEG_FILL))
            row = lax.broadcasted_iota(jnp.int32, (row_count, 128), 0)
            live[...] = jnp.where(row < length, 1.0, 0.0)
            if for_keys:
                acc[...] = jnp.zeros_like(acc)
                acc_rope[...] = jnp.zeros_like(acc_rope)

        for j in range(chips):
            own_at = pl.ds(pl.multiple_of(j * 2 * w_rows + core * w_rows, w_rows), w_rows)
            oth_at = pl.ds(pl.multiple_of(j * 2 * w_rows + (1 - core) * w_rows, w_rows), w_rows)
            for h in range(hps):
                src = slice(128 * h, 128 * h + 128)
                w_all[own_at, 256 * h:256 * h + 128] = wk_own[j, :, src]
                w_all[own_at, 256 * h + 128:256 * h + 256] = wv_own[j, :, src]
                w_all[oth_at, 256 * h:256 * h + 128] = wk_oth[j, :, src]
                w_all[oth_at, 256 * h + 128:256 * h + 256] = wv_oth[j, :, src]

        keys_lat = keys_ref[:, :LAT]
        keys_rot = keys_ref[:, LAT:]
        alive = live[...]
        lane = lax.broadcasted_iota(jnp.int32, (row_count, 128), 1)
        heads = range(hps)
        cols = [slice(128 * h, 128 * h + 128) for h in heads]
        both = [dot(keys_lat, w_all[:, 256 * h:256 * h + 256], ((1,), (0,))).astype(BF) for h in heads]
        value = [b[:, 128:] for b in both]
        key_full = [jnp.concatenate([b[:, :128], keys_rot], axis=1) for b in both]
        query = []
        for h in heads:
            mine = (lane < 64) if h % 2 == 0 else (lane >= 64)
            rope = jnp.where(mine, qr_ref[:, 128 * (h // 2):128 * (h // 2) + 128].astype(F32), 0.0).astype(BF)
            query.append(jnp.concatenate([qn_ref[:, cols[h]], rope], axis=1))
        grad_out = [(og_ref[:, c].astype(F32) * alive).astype(BF) for c in cols]
        scores = [dot(key_full[h], query[h], ((1,), (1,))) + bias[...] for h in heads]
        grad_prob = [dot(value[h], grad_out[h], ((1,), (1,))) for h in heads]
        prob_half, grad_score = [], []
        for h in heads:
            top = jnp.max(scores[h], axis=0, keepdims=True)
            raised = jnp.exp2((scores[h] - top) * exp_scale)
            prob = raised * (1.0 / jnp.sum(raised, axis=0, keepdims=True))
            prob_half.append(prob.astype(BF))
            weighed = prob * grad_prob[h]
            inner = jnp.sum(weighed, axis=0, keepdims=True)
            grad_score.append(((weighed - prob * inner) * scale).astype(BF))
        if not for_keys:
            attn = [dot(prob_half[h], value[h], ((0,), (0,))) for h in heads]
            grad_query = [dot(grad_score[h], key_full[h], ((0,), (0,))) for h in heads]
            for h in heads:
                out_ref[:, cols[h]] = (attn[h] * alive).astype(BF)
                gqn_ref[:, cols[h]] = grad_query[h][:, :128].astype(BF)
                if h % 2 == 1:
                    gqr_ref[:, cols[h // 2]] = jnp.where(
                        lane < 64, grad_query[h - 1][:, 128:], grad_query[h][:, 128:]).astype(BF)
            return
        grad_key = [dot(grad_score[h], query[h], ((1,), (0,))) for h in heads]
        grad_value = [dot(prob_half[h], grad_out[h], ((1,), (0,))) for h in heads]
        grads = []
        rope_sum = None
        for h in heads:
            grads += [grad_key[h][:, :128].astype(BF), grad_value[h].astype(BF)]
            rope_sum = grad_key[h][:, 128:] if rope_sum is None else rope_sum + grad_key[h][:, 128:]
        acc[...] += dot(jnp.concatenate(grads, axis=1), w_all[...], ((1,), (1,)))
        acc_rope[...] += rope_sum

        @pl.when(step == steps - 1)
        def _():
            rope = acc_rope[...]
            acc_rope[...] = rope + pltpu.roll(rope, 64, 1)
            low = lax.broadcasted_iota(jnp.int32, (owned, 128), 1) < 64
            for owner in range(ctx_count):
                at = pl.ds(pl.multiple_of(block_of(jnp.bitwise_xor(ctx, owner)) * owned, owned), owned)
                first = prompt_count + (owner % 4) * resp_owned
                resp_at = slice(first, first + resp_owned)
                terms_ref[owner, :, :LAT] = acc[at, :].astype(BF)
                terms_ref[owner, :, LAT:2 * LAT] = acc[resp_at, :].astype(BF)
                terms_ref[owner, :, 2 * LAT:] = jnp.where(low, acc_rope[at, :], acc_rope[resp_at, :]).astype(BF)

    wide = 128 * hps
    return pl.pallas_call(
        kernel,
        grid=(steps,),
        in_specs=[
            pl.BlockSpec(memory_space=pltpu.SMEM),
            pl.BlockSpec((row_count, wide), lambda i: (0, i)),
            pl.BlockSpec((row_count, wide // 2), lambda i: (0, i)),
            pl.BlockSpec((row_count, wide), lambda i: (0, i)),
            pl.BlockSpec((key_count, WIDE), lambda i: (0, 0)),
            pl.BlockSpec((chips, w_rows, wide), lambda i: (0, 0, i)),
            pl.BlockSpec((chips, w_rows, wide), lambda i: (0, 1, i)),
            pl.BlockSpec((chips, w_rows, wide), lambda i: (0, 0, i)),
            pl.BlockSpec((chips, w_rows, wide), lambda i: (0, 1, i)),
        ],
        out_specs=pl.BlockSpec((ctx_count, owned, 2 * LAT + 128), lambda i: (0, 0, 0)) if for_keys else [
            pl.BlockSpec((row_count, wide), lambda i: (0, i)),
            pl.BlockSpec((row_count, wide), lambda i: (0, i)),
            pl.BlockSpec((row_count, wide // 2), lambda i: (0, i)),
        ],
        out_shape=pltpu.HBM((ctx_count, owned, 2 * LAT + 128), BF) if for_keys else [
            jax.ShapeDtypeStruct(q_nope.shape, BF),
            jax.ShapeDtypeStruct(q_nope.shape, BF),
            jax.ShapeDtypeStruct(q_rope.shape, BF),
        ],
        scratch_shapes=[
            pltpu.VMEM((LAT, 256 * hps), BF),
            pltpu.VMEM((key_count, row_count), F32),
            pltpu.VMEM((row_count, 128), F32),
        ] + ([pltpu.VMEM((key_count, LAT), F32), pltpu.VMEM((key_count, 128), F32)] if for_keys else []),
        compiler_params=pltpu.CompilerParams(vmem_limit_bytes=(58 if for_keys else 28) * 2**20),
        cost_estimate=pl.CostEstimate(flops=6 * 10**9, bytes_accessed=8 * 2**20, transcendentals=2048 * 384),
        name="key_terms" if for_keys else "attention",
    )(facts, q_nope, q_rope, out_grad, keys, w_own, w_own, w_other, w_other)


def add_heads(terms, copies):
    owned = terms.shape[1]

    def kernel(terms_ref, prompt_ref, resp_ref, held, sems):
        def total(at):
            result = terms_ref[0, :, at].astype(F32)
            for j in range(1, terms.shape[0]):
                result = result + terms_ref[j, :, at].astype(F32)
            return result.astype(BF)

        rope = total(slice(2 * LAT, 2 * LAT + 128))
        held[:, :LAT] = total(slice(0, LAT))
        held[:, LAT:] = rope
        moves = [pltpu.make_async_copy(held, prompt_ref.at[j], sems.at[j]) for j in range(copies)]
        for move in moves:
            move.start()
        resp_ref[:, :LAT] = total(slice(LAT, 2 * LAT))
        resp_ref[:, LAT:] = rope
        for move in moves:
            move.wait()

    return pl.pallas_call(
        kernel,
        in_specs=[pl.BlockSpec(memory_space=pltpu.VMEM)],
        out_specs=[pl.BlockSpec(memory_space=pl.ANY), pl.BlockSpec(memory_space=pltpu.VMEM)],
        out_shape=[
            pltpu.HBM((copies, owned, WIDE), BF),
            jax.ShapeDtypeStruct((owned, WIDE), BF),
        ],
        scratch_shapes=[pltpu.VMEM((owned, WIDE), BF), pltpu.SemaphoreType.DMA((copies,))],
        compiler_params=pltpu.CompilerParams(vmem_limit_bytes=4 * 2**20),
        name="add_heads",
    )(terms)


def finish(facts, prompt_terms, resp_pieces):
    samples, owned, _ = prompt_terms.shape
    piece_rows = resp_pieces[0].shape[0]
    row_count = piece_rows * len(resp_pieces)
    def kernel(facts_ref, prompt_ref, piece_0, piece_1, piece_2, piece_3, plat_ref, prot_ref, rlat_ref, rrot_ref, held):
        ctx = facts_ref[2]
        total = prompt_ref[0].astype(F32)
        for j in range(1, samples):
            total = total + prompt_ref[j].astype(F32)
        plat_ref[...] = total[:, :LAT]
        prot_ref[...] = total[:, LAT:LAT + 64]
        for distance, piece in enumerate((piece_0, piece_1, piece_2, piece_3)):
            start = jnp.bitwise_xor(jnp.bitwise_and(ctx, 3), distance) * piece_rows
            at = pl.ds(pl.multiple_of(start, piece_rows), piece_rows)
            rows = piece[...].astype(F32)
            rlat_ref[at, :] = rows[:, :LAT]
            held[at, :] = rows[:, LAT:]
        turned = jnp.swapaxes(held[...], 0, 1)
        rrot_ref[...] = turned[64:]

    vm = pl.BlockSpec(memory_space=pltpu.VMEM)
    return pl.pallas_call(
        kernel,
        in_specs=[pl.BlockSpec(memory_space=pltpu.SMEM)] + [vm] * 5,
        out_specs=[vm] * 4,
        out_shape=[
            jax.ShapeDtypeStruct((owned, LAT), F32),
            jax.ShapeDtypeStruct((owned, 64), F32),
            jax.ShapeDtypeStruct((row_count, LAT), F32),
            jax.ShapeDtypeStruct((64, row_count), F32),
        ],
        scratch_shapes=[pltpu.VMEM((row_count, 128), F32)],
        compiler_params=pltpu.CompilerParams(vmem_limit_bytes=4 * 2**20),
        name="finish",
    )(facts, prompt_terms, *resp_pieces)


def from_distance(block, distance):
    return lax.ppermute(block, "ctx", [(i, i ^ distance) for i in range(8)])


def meet(block):
    return jnp.concatenate([block, from_distance(block, 4)], axis=0)


def share(block):
    return [block] + [from_distance(block, distance) for distance in (3, 2, 1)][::-1]


def per_device(
    q_nope,
    q_rope,
    prompt_latent,
    prompt_rope,
    resp_latent,
    resp_rope,
    w_key,
    w_value,
    out_grad,
    lengths,
    offsets,
):
    ctx = lax.axis_index("ctx").astype(jnp.int32)
    core = jnp.bitwise_and(lax.axis_index("sample").astype(jnp.int32), 1)
    facts = jnp.concatenate([lengths, offsets, ctx[None], core[None]])
    same_core = [[2 * chip + c for chip in range(8)] for c in range(2)]
    w_own = lax.all_to_all(
        spread_weights(w_key, w_value, 8), "sample", 0, 0, tiled=True, axis_index_groups=same_core)
    prompt_pieces = share(meet(jnp.concatenate([prompt_latent, prompt_rope, prompt_rope], axis=1)))
    keys = join_keys(prompt_pieces, resp_latent, resp_rope)
    w_own, keys = lax.optimization_barrier((w_own, keys))
    w_other = lax.ppermute(w_own, "sample", [(i, i ^ 1) for i in range(16)])
    held = (q_nope, q_rope, out_grad, keys, w_own, w_other)
    terms, later_facts = lax.optimization_barrier((attention(True, facts, *held), facts))
    attn_out, grad_query_nope, grad_query_rope = attention(False, later_facts, *held)
    terms, attn_out, grad_query_nope, grad_query_rope = lax.optimization_barrier(
        (lax.all_to_all(terms, "ctx", 0, 0, tiled=True), attn_out, grad_query_nope, grad_query_rope))
    prompt_part, resp_part = add_heads(terms, 16)
    prompt_part = lax.all_to_all(prompt_part, "sample", 0, 0, tiled=True)
    resp_pieces = share(resp_part)
    prompt_lat, prompt_rot, resp_lat, resp_rot = finish(facts, prompt_part, resp_pieces)
    return (attn_out, grad_query_nope, grad_query_rope, prompt_lat, prompt_rot, resp_lat, resp_rot.T)


def solution(mesh):
    placed = (
        P(("group", "sample"), "ctx"),
        P(("group", "sample"), "ctx"),
        P(("group", "ctx"), None),
        P(("group", "ctx"), None),
        P(("group", "sample"), None),
        P(("group", "sample"), None),
        P("sample", "ctx"),
        P("sample", "ctx"),
        P(("group", "sample"), "ctx"),
        P(("group", "sample")),
        P(("group", "sample")),
    )
    return jax.shard_map(
        per_device,
        mesh=mesh,
        in_specs=placed,
        out_specs=(
            P(("group", "sample"), "ctx"),
            P(("group", "sample"), "ctx"),
            P(("group", "sample"), "ctx"),
            P(("group", "ctx"), None),
            P(("group", "ctx"), None),
            P(("group", "sample"), None),
            P(("group", "sample"), None),
        ),
        check_vma=False,
    )
```

```python
import math

import jax
import jax.numpy as jnp
from jax import lax
from jax.experimental import pallas as pl
from jax.experimental.pallas import tpu as pltpu
from jax.sharding import PartitionSpec as P

NEG_FILL = -1e30
HEADS_PER_STEP = 8
LAT = 512
WIDE = 640
BF = jnp.bfloat16
F32 = jnp.float32


def spread_weights(w_key, w_value, copies):
    rows, cols = w_key.shape

    def kernel(key_ref, value_ref, out_ref, held, sems):
        moves = [
            pltpu.make_async_copy(key_ref, held.at[pl.ds(0, rows)], sems.at[0]),
            pltpu.make_async_copy(value_ref, held.at[pl.ds(rows, rows)], sems.at[1]),
        ]
        for move in moves:
            move.start()
        sent = []
        for k, move in enumerate(moves):
            move.wait()
            at = pl.ds(k * rows, rows)
            for j in range(copies):
                sent.append(pltpu.make_async_copy(held.at[at], out_ref.at[j, at], sems.at[2 + k * copies + j]))
                sent[-1].start()
        for move in sent:
            move.wait()

    return pl.pallas_call(
        kernel,
        out_shape=pltpu.HBM((copies, 2 * rows, cols), BF),
        in_specs=[pl.BlockSpec(memory_space=pltpu.HBM)] * 2,
        out_specs=pl.BlockSpec(memory_space=pl.ANY),
        scratch_shapes=[pltpu.VMEM((2 * rows, cols), BF), pltpu.SemaphoreType.DMA((2 + 2 * copies,))],
        compiler_params=pltpu.CompilerParams(vmem_limit_bytes=58 * 2**20),
        name="spread_weights",
    )(w_key, w_value)


def block_of(distance):
    return 2 * jnp.bitwise_and(distance, 3) + lax.shift_right_logical(distance, 2)


def dot(left, right, dims):
    return lax.dot_general(left, right, (dims, ((), ())), preferred_element_type=F32)


def join_keys(pieces, resp_latent, resp_rope):
    piece_rows = pieces[0].shape[0]
    prompt_count = piece_rows * len(pieces)
    key_count = prompt_count + resp_latent.shape[0]

    def kernel(piece_0, piece_1, piece_2, piece_3, lat_ref, rot_ref, keys_ref):
        for j, piece in enumerate((piece_0, piece_1, piece_2, piece_3)):
            keys_ref[j * piece_rows:(j + 1) * piece_rows] = piece[...]
        keys_ref[prompt_count:, :LAT] = lat_ref[...]
        turned = rot_ref[...].astype(F32)
        turned = jnp.concatenate([turned, turned], axis=0)
        keys_ref[prompt_count:, LAT:] = jnp.swapaxes(turned, 0, 1).astype(BF)

    return pl.pallas_call(
        kernel,
        in_specs=[pl.BlockSpec(memory_space=pltpu.VMEM)] * 6,
        out_specs=pl.BlockSpec(memory_space=pltpu.VMEM),
        out_shape=pltpu.HBM((key_count, WIDE), BF),
        compiler_params=pltpu.CompilerParams(vmem_limit_bytes=4 * 2**20),
        name="join_keys",
    )(*pieces, resp_latent, resp_rope.T)


def attention(for_keys, facts, q_nope, q_rope, out_grad, keys, w_own, w_other):
    row_count = q_nope.shape[0]
    key_count = keys.shape[0]
    prompt_count = key_count - row_count
    head_count = q_nope.shape[1] // 128
    hps = HEADS_PER_STEP
    steps = head_count // hps
    chips, two_rows, _ = w_own.shape
    w_rows = two_rows // 2
    ctx_count = 8
    owned = prompt_count // ctx_count
    resp_owned = row_count // 4
    scale = 1.0 / math.sqrt(192.0)
    exp_scale = scale * math.log2(math.e)

    def kernel(facts_ref, qn_ref, qr_ref, og_ref, keys_ref, wk_own, wv_own, wk_oth, wv_oth, *refs):
        if for_keys:
            terms_ref, w_all, bias, live, acc, acc_rope = refs
        else:
            out_ref, gqn_ref, gqr_ref, w_all, bias, live = refs
        step = pl.program_id(0)
        length, offset, ctx, core = facts_ref[0], facts_ref[1], facts_ref[2], facts_ref[3]

        @pl.when(step == 0)
        def _():
            key = lax.broadcasted_iota(jnp.int32, (key_count, row_count), 0)
            slot = lax.broadcasted_iota(jnp.int32, (key_count, row_count), 1)
            block = lax.shift_right_logical(key, 5)
            distance = lax.shift_right_logical(block, 1) + 4 * jnp.bitwise_and(block, 1)
            place = jnp.bitwise_xor(distance, ctx) * owned + jnp.bitwise_and(key, owned - 1)
            bias[...] = jnp.where(
                key < prompt_count,
                jnp.where(place < offset, 0.0, NEG_FILL),
                jnp.where(key - prompt_count <= slot, 0.0, NEG_FILL))
            row = lax.broadcasted_iota(jnp.int32, (row_count, 128), 0)
            live[...] = jnp.where(row < length, 1.0, 0.0)
            if for_keys:
                acc[...] = jnp.zeros_like(acc)
                acc_rope[...] = jnp.zeros_like(acc_rope)

        for j in range(chips):
            own_at = pl.ds(pl.multiple_of(j * 2 * w_rows + core * w_rows, w_rows), w_rows)
            oth_at = pl.ds(pl.multiple_of(j * 2 * w_rows + (1 - core) * w_rows, w_rows), w_rows)
            for h in range(hps):
                src = slice(128 * h, 128 * h + 128)
                w_all[own_at, 256 * h:256 * h + 128] = wk_own[j, :, src]
                w_all[own_at, 256 * h + 128:256 * h + 256] = wv_own[j, :, src]
                w_all[oth_at, 256 * h:256 * h + 128] = wk_oth[j, :, src]
                w_all[oth_at, 256 * h + 128:256 * h + 256] = wv_oth[j, :, src]

        keys_lat = keys_ref[:, :LAT]
        keys_rot = keys_ref[:, LAT:]
        alive = live[...]
        lane = lax.broadcasted_iota(jnp.int32, (row_count, 128), 1)
        heads = range(hps)
        cols = [slice(128 * h, 128 * h + 128) for h in heads]
        both = [dot(keys_lat, w_all[:, 256 * h:256 * h + 256], ((1,), (0,))).astype(BF) for h in heads]
        value = [b[:, 128:] for b in both]
        key_full = [jnp.concatenate([b[:, :128], keys_rot], axis=1) for b in both]
        query = []
        for h in heads:
            mine = (lane < 64) if h % 2 == 0 else (lane >= 64)
            rope = jnp.where(mine, qr_ref[:, 128 * (h // 2):128 * (h // 2) + 128].astype(F32), 0.0).astype(BF)
            query.append(jnp.concatenate([qn_ref[:, cols[h]], rope], axis=1))
        grad_out = [(og_ref[:, c].astype(F32) * alive).astype(BF) for c in cols]
        scores = [dot(key_full[h], query[h], ((1,), (1,))) + bias[...] for h in heads]
        blank = jnp.zeros((row_count, 128), BF)
        grad_pair = [
            jnp.concatenate(
                [jnp.concatenate([grad_out[h], blank], axis=1), jnp.concatenate([blank, grad_out[h + 1]], axis=1)], axis=0)
            for h in heads[::2]]
        grad_prob = []
        for h in heads[::2]:
            pair = dot(jnp.concatenate(value[h:h + 2], axis=1), grad_pair[h // 2], ((1,), (1,)))
            grad_prob += [pair[:, :row_count], pair[:, row_count:]]
        prob_half, grad_score = [], []
        for h in heads:
            top = jnp.max(scores[h], axis=0, keepdims=True)
            raised = jnp.exp2((scores[h] - top) * exp_scale)
            prob = raised * (1.0 / jnp.sum(raised, axis=0, keepdims=True))
            prob_half.append(prob.astype(BF))
            weighed = prob * grad_prob[h]
            inner = jnp.sum(weighed, axis=0, keepdims=True)
            grad_score.append(((weighed - prob * inner) * scale).astype(BF))
        if not for_keys:
            attn = [dot(prob_half[h], value[h], ((0,), (0,))) for h in heads]
            grad_query = [dot(grad_score[h], key_full[h], ((0,), (0,))) for h in heads]
            for h in heads:
                out_ref[:, cols[h]] = (attn[h] * alive).astype(BF)
                gqn_ref[:, cols[h]] = grad_query[h][:, :128].astype(BF)
                if h % 2 == 1:
                    gqr_ref[:, cols[h // 2]] = jnp.where(
                        lane < 64, grad_query[h - 1][:, 128:], grad_query[h][:, 128:]).astype(BF)
            return
        grad_key = [dot(grad_score[h], query[h], ((1,), (0,))) for h in heads]
        grad_value = []
        for h in heads[::2]:
            pair = dot(jnp.concatenate(prob_half[h:h + 2], axis=1), grad_pair[h // 2], ((1,), (0,)))
            grad_value += [pair[:, :128], pair[:, 128:]]
        grads = []
        rope_sum = None
        for h in heads:
            grads += [grad_key[h][:, :128].astype(BF), grad_value[h].astype(BF)]
            rope_sum = grad_key[h][:, 128:] if rope_sum is None else rope_sum + grad_key[h][:, 128:]
        acc[...] += dot(jnp.concatenate(grads, axis=1), w_all[...], ((1,), (1,)))
        acc_rope[...] += rope_sum

        @pl.when(step == steps - 1)
        def _():
            rope = acc_rope[...]
            acc_rope[...] = rope + pltpu.roll(rope, 64, 1)
            low = lax.broadcasted_iota(jnp.int32, (owned, 128), 1) < 64
            for owner in range(ctx_count):
                at = pl.ds(pl.multiple_of(block_of(jnp.bitwise_xor(ctx, owner)) * owned, owned), owned)
                first = prompt_count + (owner % 4) * resp_owned
                resp_at = slice(first, first + resp_owned)
                terms_ref[owner, :, :LAT] = acc[at, :].astype(BF)
                terms_ref[owner, :, LAT:2 * LAT] = acc[resp_at, :].astype(BF)
                terms_ref[owner, :, 2 * LAT:] = jnp.where(low, acc_rope[at, :], acc_rope[resp_at, :]).astype(BF)

    wide = 128 * hps
    return pl.pallas_call(
        kernel,
        grid=(steps,),
        in_specs=[
            pl.BlockSpec(memory_space=pltpu.SMEM),
            pl.BlockSpec((row_count, wide), lambda i: (0, i)),
            pl.BlockSpec((row_count, wide // 2), lambda i: (0, i)),
            pl.BlockSpec((row_count, wide), lambda i: (0, i)),
            pl.BlockSpec((key_count, WIDE), lambda i: (0, 0)),
            pl.BlockSpec((chips, w_rows, wide), lambda i: (0, 0, i)),
            pl.BlockSpec((chips, w_rows, wide), lambda i: (0, 1, i)),
            pl.BlockSpec((chips, w_rows, wide), lambda i: (0, 0, i)),
            pl.BlockSpec((chips, w_rows, wide), lambda i: (0, 1, i)),
        ],
        out_specs=pl.BlockSpec((ctx_count, owned, 2 * LAT + 128), lambda i: (0, 0, 0)) if for_keys else [
            pl.BlockSpec((row_count, wide), lambda i: (0, i)),
            pl.BlockSpec((row_count, wide), lambda i: (0, i)),
            pl.BlockSpec((row_count, wide // 2), lambda i: (0, i)),
        ],
        out_shape=pltpu.HBM((ctx_count, owned, 2 * LAT + 128), BF) if for_keys else [
            jax.ShapeDtypeStruct(q_nope.shape, BF),
            jax.ShapeDtypeStruct(q_nope.shape, BF),
            jax.ShapeDtypeStruct(q_rope.shape, BF),
        ],
        scratch_shapes=[
            pltpu.VMEM((LAT, 256 * hps), BF),
            pltpu.VMEM((key_count, row_count), F32),
            pltpu.VMEM((row_count, 128), F32),
        ] + ([pltpu.VMEM((key_count, LAT), F32), pltpu.VMEM((key_count, 128), F32)] if for_keys else []),
        compiler_params=pltpu.CompilerParams(vmem_limit_bytes=(58 if for_keys else 28) * 2**20),
        cost_estimate=pl.CostEstimate(flops=6 * 10**9, bytes_accessed=8 * 2**20, transcendentals=2048 * 384),
        name="key_terms" if for_keys else "attention",
    )(facts, q_nope, q_rope, out_grad, keys, w_own, w_own, w_other, w_other)


def add_heads(terms, copies):
    owned = terms.shape[1]

    def kernel(terms_ref, prompt_ref, resp_ref, held, sems):
        def total(at):
            result = terms_ref[0, :, at].astype(F32)
            for j in range(1, terms.shape[0]):
                result = result + terms_ref[j, :, at].astype(F32)
            return result.astype(BF)

        rope = total(slice(2 * LAT, 2 * LAT + 128))
        held[:, :LAT] = total(slice(0, LAT))
        held[:, LAT:] = rope
        moves = [pltpu.make_async_copy(held, prompt_ref.at[j], sems.at[j]) for j in range(copies)]
        for move in moves:
            move.start()
        resp_ref[:, :LAT] = total(slice(LAT, 2 * LAT))
        resp_ref[:, LAT:] = rope
        for move in moves:
            move.wait()

    return pl.pallas_call(
        kernel,
        in_specs=[pl.BlockSpec(memory_space=pltpu.VMEM)],
        out_specs=[pl.BlockSpec(memory_space=pl.ANY), pl.BlockSpec(memory_space=pltpu.VMEM)],
        out_shape=[
            pltpu.HBM((copies, owned, WIDE), BF),
            jax.ShapeDtypeStruct((owned, WIDE), BF),
        ],
        scratch_shapes=[pltpu.VMEM((owned, WIDE), BF), pltpu.SemaphoreType.DMA((copies,))],
        compiler_params=pltpu.CompilerParams(vmem_limit_bytes=4 * 2**20),
        name="add_heads",
    )(terms)


def finish(facts, prompt_terms, resp_pieces):
    samples, owned, _ = prompt_terms.shape
    piece_rows = resp_pieces[0].shape[0]
    row_count = piece_rows * len(resp_pieces)
    def kernel(facts_ref, prompt_ref, piece_0, piece_1, piece_2, piece_3, plat_ref, prot_ref, rlat_ref, rrot_ref, held):
        ctx = facts_ref[2]
        total = prompt_ref[0].astype(F32)
        for j in range(1, samples):
            total = total + prompt_ref[j].astype(F32)
        plat_ref[...] = total[:, :LAT]
        prot_ref[...] = total[:, LAT:LAT + 64]
        for distance, piece in enumerate((piece_0, piece_1, piece_2, piece_3)):
            start = jnp.bitwise_xor(jnp.bitwise_and(ctx, 3), distance) * piece_rows
            at = pl.ds(pl.multiple_of(start, piece_rows), piece_rows)
            rows = piece[...].astype(F32)
            rlat_ref[at, :] = rows[:, :LAT]
            held[at, :] = rows[:, LAT:]
        turned = jnp.swapaxes(held[...], 0, 1)
        rrot_ref[...] = turned[64:]

    vm = pl.BlockSpec(memory_space=pltpu.VMEM)
    return pl.pallas_call(
        kernel,
        in_specs=[pl.BlockSpec(memory_space=pltpu.SMEM)] + [vm] * 5,
        out_specs=[vm] * 4,
        out_shape=[
            jax.ShapeDtypeStruct((owned, LAT), F32),
            jax.ShapeDtypeStruct((owned, 64), F32),
            jax.ShapeDtypeStruct((row_count, LAT), F32),
            jax.ShapeDtypeStruct((64, row_count), F32),
        ],
        scratch_shapes=[pltpu.VMEM((row_count, 128), F32)],
        compiler_params=pltpu.CompilerParams(vmem_limit_bytes=4 * 2**20),
        name="finish",
    )(facts, prompt_terms, *resp_pieces)


def from_distance(block, distance):
    return lax.ppermute(block, "ctx", [(i, i ^ distance) for i in range(8)])


def meet(block):
    return jnp.concatenate([block, from_distance(block, 4)], axis=0)


def share(block):
    return [block] + [from_distance(block, distance) for distance in (3, 2, 1)][::-1]


def per_device(
    q_nope,
    q_rope,
    prompt_latent,
    prompt_rope,
    resp_latent,
    resp_rope,
    w_key,
    w_value,
    out_grad,
    lengths,
    offsets,
):
    ctx = lax.axis_index("ctx").astype(jnp.int32)
    core = jnp.bitwise_and(lax.axis_index("sample").astype(jnp.int32), 1)
    facts = jnp.concatenate([lengths, offsets, ctx[None], core[None]])
    same_core = [[2 * chip + c for chip in range(8)] for c in range(2)]
    w_own = lax.all_to_all(
        spread_weights(w_key, w_value, 8), "sample", 0, 0, tiled=True, axis_index_groups=same_core)
    prompt_pieces = share(meet(jnp.concatenate([prompt_latent, prompt_rope, prompt_rope], axis=1)))
    keys = join_keys(prompt_pieces, resp_latent, resp_rope)
    w_own, keys = lax.optimization_barrier((w_own, keys))
    w_other = lax.ppermute(w_own, "sample", [(i, i ^ 1) for i in range(16)])
    held = (q_nope, q_rope, out_grad, keys, w_own, w_other)
    terms, later_facts = lax.optimization_barrier((attention(True, facts, *held), facts))
    attn_out, grad_query_nope, grad_query_rope = attention(False, later_facts, *held)
    terms, attn_out, grad_query_nope, grad_query_rope = lax.optimization_barrier(
        (lax.all_to_all(terms, "ctx", 0, 0, tiled=True), attn_out, grad_query_nope, grad_query_rope))
    prompt_part, resp_part = add_heads(terms, 16)
    prompt_part = lax.all_to_all(prompt_part, "sample", 0, 0, tiled=True)
    resp_pieces = share(resp_part)
    prompt_lat, prompt_rot, resp_lat, resp_rot = finish(facts, prompt_part, resp_pieces)
    return (attn_out, grad_query_nope, grad_query_rope, prompt_lat, prompt_rot, resp_lat, resp_rot.T)


def solution(mesh):
    placed = (
        P(("group", "sample"), "ctx"),
        P(("group", "sample"), "ctx"),
        P(("group", "ctx"), None),
        P(("group", "ctx"), None),
        P(("group", "sample"), None),
        P(("group", "sample"), None),
        P("sample", "ctx"),
        P("sample", "ctx"),
        P(("group", "sample"), "ctx"),
        P(("group", "sample")),
        P(("group", "sample")),
    )
    return jax.shard_map(
        per_device,
        mesh=mesh,
        in_specs=placed,
        out_specs=(
            P(("group", "sample"), "ctx"),
            P(("group", "sample"), "ctx"),
            P(("group", "sample"), "ctx"),
            P(("group", "ctx"), None),
            P(("group", "ctx"), None),
            P(("group", "sample"), None),
            P(("group", "sample"), None),
        ),
        check_vma=False,
    )
```

```python
import math

import jax
import jax.numpy as jnp
from jax import lax
from jax.experimental import pallas as pl
from jax.experimental.pallas import tpu as pltpu
from jax.sharding import PartitionSpec as P

NEG_FILL = -1e30
HEADS_PER_STEP = 8
LAT = 512
WIDE = 640
BF = jnp.bfloat16
F32 = jnp.float32


def spread_weights(w_key, w_value, copies):
    rows, cols = w_key.shape

    def kernel(key_ref, value_ref, out_ref, held, sems):
        moves = [
            pltpu.make_async_copy(key_ref, held.at[pl.ds(0, rows)], sems.at[0]),
            pltpu.make_async_copy(value_ref, held.at[pl.ds(rows, rows)], sems.at[1]),
        ]
        for move in moves:
            move.start()
        sent = []
        for k, move in enumerate(moves):
            move.wait()
            at = pl.ds(k * rows, rows)
            for j in range(copies):
                sent.append(pltpu.make_async_copy(held.at[at], out_ref.at[j, at], sems.at[2 + k * copies + j]))
                sent[-1].start()
        for move in sent:
            move.wait()

    return pl.pallas_call(
        kernel,
        out_shape=pltpu.HBM((copies, 2 * rows, cols), BF),
        in_specs=[pl.BlockSpec(memory_space=pltpu.HBM)] * 2,
        out_specs=pl.BlockSpec(memory_space=pl.ANY),
        scratch_shapes=[pltpu.VMEM((2 * rows, cols), BF), pltpu.SemaphoreType.DMA((2 + 2 * copies,))],
        compiler_params=pltpu.CompilerParams(vmem_limit_bytes=58 * 2**20),
        name="spread_weights",
    )(w_key, w_value)


def block_of(distance):
    return 2 * jnp.bitwise_and(distance, 3) + lax.shift_right_logical(distance, 2)


def dot(left, right, dims):
    return lax.dot_general(left, right, (dims, ((), ())), preferred_element_type=F32)


def join_keys(pieces, resp_latent, resp_rope):
    piece_rows = pieces[0].shape[0]
    prompt_count = piece_rows * len(pieces)
    key_count = prompt_count + resp_latent.shape[0]

    def kernel(piece_0, piece_1, piece_2, piece_3, lat_ref, rot_ref, keys_ref):
        for j, piece in enumerate((piece_0, piece_1, piece_2, piece_3)):
            keys_ref[j * piece_rows:(j + 1) * piece_rows] = piece[...]
        keys_ref[prompt_count:, :LAT] = lat_ref[...]
        turned = rot_ref[...].astype(F32)
        turned = jnp.concatenate([turned, turned], axis=0)
        keys_ref[prompt_count:, LAT:] = jnp.swapaxes(turned, 0, 1).astype(BF)

    return pl.pallas_call(
        kernel,
        in_specs=[pl.BlockSpec(memory_space=pltpu.VMEM)] * 6,
        out_specs=pl.BlockSpec(memory_space=pltpu.VMEM),
        out_shape=pltpu.HBM((key_count, WIDE), BF),
        compiler_params=pltpu.CompilerParams(vmem_limit_bytes=4 * 2**20),
        name="join_keys",
    )(*pieces, resp_latent, resp_rope.T)


def attention(for_keys, facts, q_nope, q_rope, out_grad, keys, w_own, w_other):
    row_count = q_nope.shape[0]
    key_count = keys.shape[0]
    prompt_count = key_count - row_count
    head_count = q_nope.shape[1] // 128
    hps = HEADS_PER_STEP
    steps = head_count // hps
    chips, two_rows, _ = w_own.shape
    w_rows = two_rows // 2
    ctx_count = 8
    owned = prompt_count // ctx_count
    resp_owned = row_count // 4
    scale = 1.0 / math.sqrt(192.0)
    exp_scale = scale * math.log2(math.e)

    def kernel(facts_ref, qn_ref, qr_ref, og_ref, keys_ref, wk_own, wv_own, wk_oth, wv_oth, *refs):
        if for_keys:
            terms_ref, w_all, bias, live, acc, acc_rope = refs
        else:
            out_ref, gqn_ref, gqr_ref, w_all, bias, live = refs
        step = pl.program_id(0)
        length, offset, ctx, core = facts_ref[0], facts_ref[1], facts_ref[2], facts_ref[3]

        @pl.when(step == 0)
        def _():
            key = lax.broadcasted_iota(jnp.int32, (key_count, row_count), 0)
            slot = lax.broadcasted_iota(jnp.int32, (key_count, row_count), 1)
            block = lax.shift_right_logical(key, 5)
            distance = lax.shift_right_logical(block, 1) + 4 * jnp.bitwise_and(block, 1)
            place = jnp.bitwise_xor(distance, ctx) * owned + jnp.bitwise_and(key, owned - 1)
            bias[...] = jnp.where(
                key < prompt_count,
                jnp.where(place < offset, 0.0, NEG_FILL),
                jnp.where(key - prompt_count <= slot, 0.0, NEG_FILL))
            row = lax.broadcasted_iota(jnp.int32, (row_count, 128), 0)
            live[...] = jnp.where(row < length, 1.0, 0.0)
            if for_keys:
                acc[...] = jnp.zeros_like(acc)
                acc_rope[...] = jnp.zeros_like(acc_rope)

        for j in range(chips):
            own_at = pl.ds(pl.multiple_of(j * 2 * w_rows + core * w_rows, w_rows), w_rows)
            oth_at = pl.ds(pl.multiple_of(j * 2 * w_rows + (1 - core) * w_rows, w_rows), w_rows)
            for h in range(hps):
                src = slice(128 * h, 128 * h + 128)
                w_all[own_at, 256 * h:256 * h + 128] = wk_own[j, :, src]
                w_all[own_at, 256 * h + 128:256 * h + 256] = wv_own[j, :, src]
                w_all[oth_at, 256 * h:256 * h + 128] = wk_oth[j, :, src]
                w_all[oth_at, 256 * h + 128:256 * h + 256] = wv_oth[j, :, src]

        keys_lat = keys_ref[:, :LAT]
        keys_rot = keys_ref[:, LAT:]
        alive = live[...]
        lane = lax.broadcasted_iota(jnp.int32, (row_count, 128), 1)
        heads = range(hps)
        cols = [slice(128 * h, 128 * h + 128) for h in heads]
        both = [dot(keys_lat, w_all[:, 256 * h:256 * h + 256], ((1,), (0,))).astype(BF) for h in heads]
        value = [b[:, 128:] for b in both]
        key_full = [jnp.concatenate([b[:, :128], keys_rot], axis=1) for b in both]
        query = []
        for h in heads:
            mine = (lane < 64) if h % 2 == 0 else (lane >= 64)
            rope = jnp.where(mine, qr_ref[:, 128 * (h // 2):128 * (h // 2) + 128].astype(F32), 0.0).astype(BF)
            query.append(jnp.concatenate([qn_ref[:, cols[h]], rope], axis=1))
        grad_out = [(og_ref[:, c].astype(F32) * alive).astype(BF) for c in cols]
        scores = [dot(key_full[h], query[h], ((1,), (1,))) + bias[...] for h in heads]
        blank = jnp.zeros((row_count, 128), BF)
        grad_pair = [
            jnp.concatenate(
                [jnp.concatenate([grad_out[h], blank], axis=1), jnp.concatenate([blank, grad_out[h + 1]], axis=1)], axis=0)
            for h in heads[::2]]
        grad_prob = []
        for h in heads[::2]:
            pair = dot(jnp.concatenate(value[h:h + 2], axis=1), grad_pair[h // 2], ((1,), (1,)))
            grad_prob += [pair[:, :row_count], pair[:, row_count:]]
        prob_half, grad_score = [], []
        for h in heads:
            top = jnp.max(scores[h], axis=0, keepdims=True)
            raised = jnp.exp2((scores[h] - top) * exp_scale)
            prob = raised * (1.0 / jnp.sum(raised, axis=0, keepdims=True))
            prob_half.append(prob.astype(BF))
            weighed = prob * grad_prob[h]
            inner = jnp.sum(weighed, axis=0, keepdims=True)
            grad_score.append(((weighed - prob * inner) * scale).astype(BF))
        if not for_keys:
            attn = [dot(prob_half[h], value[h], ((0,), (0,))) for h in heads]
            grad_query = [dot(grad_score[h], key_full[h], ((0,), (0,))) for h in heads]
            for h in heads:
                out_ref[:, cols[h]] = (attn[h] * alive).astype(BF)
                gqn_ref[:, cols[h]] = grad_query[h][:, :128].astype(BF)
                if h % 2 == 1:
                    gqr_ref[:, cols[h // 2]] = jnp.where(
                        lane < 64, grad_query[h - 1][:, 128:], grad_query[h][:, 128:]).astype(BF)
            return
        grad_key = [dot(grad_score[h], query[h], ((1,), (0,))) for h in heads]
        grad_value = []
        for h in heads[::2]:
            pair = dot(jnp.concatenate(prob_half[h:h + 2], axis=1), grad_pair[h // 2], ((1,), (0,)))
            grad_value += [pair[:, :128], pair[:, 128:]]
        grads = []
        rope_sum = None
        for h in heads:
            grads += [grad_key[h][:, :128].astype(BF), grad_value[h].astype(BF)]
            rope_sum = grad_key[h][:, 128:] if rope_sum is None else rope_sum + grad_key[h][:, 128:]
        acc[...] += dot(jnp.concatenate(grads, axis=1), w_all[...], ((1,), (1,)))
        acc_rope[...] += rope_sum

        @pl.when(step == steps - 1)
        def _():
            rope = acc_rope[...]
            acc_rope[...] = rope + pltpu.roll(rope, 64, 1)
            low = lax.broadcasted_iota(jnp.int32, (owned, 128), 1) < 64
            for owner in range(ctx_count):
                at = pl.ds(pl.multiple_of(block_of(jnp.bitwise_xor(ctx, owner)) * owned, owned), owned)
                first = prompt_count + (owner % 4) * resp_owned
                resp_at = slice(first, first + resp_owned)
                terms_ref[owner, :, :LAT] = acc[at, :].astype(BF)
                terms_ref[owner, :, LAT:2 * LAT] = acc[resp_at, :].astype(BF)
                terms_ref[owner, :, 2 * LAT:] = jnp.where(low, acc_rope[at, :], acc_rope[resp_at, :]).astype(BF)

    wide = 128 * hps
    return pl.pallas_call(
        kernel,
        grid=(steps,),
        in_specs=[
            pl.BlockSpec(memory_space=pltpu.SMEM),
            pl.BlockSpec((row_count, wide), lambda i: (0, i)),
            pl.BlockSpec((row_count, wide // 2), lambda i: (0, i)),
            pl.BlockSpec((row_count, wide), lambda i: (0, i)),
            pl.BlockSpec((key_count, WIDE), lambda i: (0, 0)),
            pl.BlockSpec((chips, w_rows, wide), lambda i: (0, 0, i)),
            pl.BlockSpec((chips, w_rows, wide), lambda i: (0, 1, i)),
            pl.BlockSpec((chips, w_rows, wide), lambda i: (0, 0, i)),
            pl.BlockSpec((chips, w_rows, wide), lambda i: (0, 1, i)),
        ],
        out_specs=pl.BlockSpec((ctx_count, owned, 2 * LAT + 128), lambda i: (0, 0, 0)) if for_keys else [
            pl.BlockSpec((row_count, wide), lambda i: (0, i)),
            pl.BlockSpec((row_count, wide), lambda i: (0, i)),
            pl.BlockSpec((row_count, wide // 2), lambda i: (0, i)),
        ],
        out_shape=pltpu.HBM((ctx_count, owned, 2 * LAT + 128), BF) if for_keys else [
            jax.ShapeDtypeStruct(q_nope.shape, BF),
            jax.ShapeDtypeStruct(q_nope.shape, BF),
            jax.ShapeDtypeStruct(q_rope.shape, BF),
        ],
        scratch_shapes=[
            pltpu.VMEM((LAT, 256 * hps), BF),
            pltpu.VMEM((key_count, row_count), F32),
            pltpu.VMEM((row_count, 128), F32),
        ] + ([pltpu.VMEM((key_count, LAT), F32), pltpu.VMEM((key_count, 128), F32)] if for_keys else []),
        compiler_params=pltpu.CompilerParams(vmem_limit_bytes=(58 if for_keys else 28) * 2**20),
        cost_estimate=pl.CostEstimate(flops=6 * 10**9, bytes_accessed=8 * 2**20, transcendentals=2048 * 384),
        name="key_terms" if for_keys else "attention",
    )(facts, q_nope, q_rope, out_grad, keys, w_own, w_own, w_other, w_other)


def add_heads(terms, copies):
    owned = terms.shape[1]

    def kernel(terms_ref, prompt_ref, resp_ref, held, sems):
        def total(at):
            result = terms_ref[0, :, at].astype(F32)
            for j in range(1, terms.shape[0]):
                result = result + terms_ref[j, :, at].astype(F32)
            return result.astype(BF)

        rope = total(slice(2 * LAT, 2 * LAT + 128))
        held[:, :LAT] = total(slice(0, LAT))
        held[:, LAT:] = rope
        moves = [pltpu.make_async_copy(held, prompt_ref.at[j], sems.at[j]) for j in range(copies)]
        for move in moves:
            move.start()
        resp_ref[:, :LAT] = total(slice(LAT, 2 * LAT))
        resp_ref[:, LAT:] = rope
        for move in moves:
            move.wait()

    return pl.pallas_call(
        kernel,
        in_specs=[pl.BlockSpec(memory_space=pltpu.VMEM)],
        out_specs=[pl.BlockSpec(memory_space=pl.ANY), pl.BlockSpec(memory_space=pltpu.VMEM)],
        out_shape=[
            pltpu.HBM((copies, owned, WIDE), BF),
            jax.ShapeDtypeStruct((owned, WIDE), BF),
        ],
        scratch_shapes=[pltpu.VMEM((owned, WIDE), BF), pltpu.SemaphoreType.DMA((copies,))],
        compiler_params=pltpu.CompilerParams(vmem_limit_bytes=4 * 2**20),
        name="add_heads",
    )(terms)


def finish(facts, prompt_terms, resp_pieces):
    samples, owned, _ = prompt_terms.shape
    piece_rows = resp_pieces[0].shape[0]
    row_count = piece_rows * len(resp_pieces)
    def kernel(facts_ref, prompt_ref, piece_0, piece_1, piece_2, piece_3, plat_ref, prot_ref, rlat_ref, rrot_ref, held):
        ctx = facts_ref[2]
        total = prompt_ref[0].astype(F32)
        for j in range(1, samples):
            total = total + prompt_ref[j].astype(F32)
        plat_ref[...] = total[:, :LAT]
        prot_ref[...] = total[:, LAT:LAT + 64]
        for distance, piece in enumerate((piece_0, piece_1, piece_2, piece_3)):
            start = jnp.bitwise_xor(jnp.bitwise_and(ctx, 3), distance) * piece_rows
            at = pl.ds(pl.multiple_of(start, piece_rows), piece_rows)
            rows = piece[...].astype(F32)
            rlat_ref[at, :] = rows[:, :LAT]
            held[at, :] = rows[:, LAT:]
        turned = jnp.swapaxes(held[...], 0, 1)
        rrot_ref[...] = turned[64:]

    vm = pl.BlockSpec(memory_space=pltpu.VMEM)
    return pl.pallas_call(
        kernel,
        in_specs=[pl.BlockSpec(memory_space=pltpu.SMEM)] + [vm] * 5,
        out_specs=[vm] * 4,
        out_shape=[
            jax.ShapeDtypeStruct((owned, LAT), F32),
            jax.ShapeDtypeStruct((owned, 64), F32),
            jax.ShapeDtypeStruct((row_count, LAT), F32),
            jax.ShapeDtypeStruct((64, row_count), F32),
        ],
        scratch_shapes=[pltpu.VMEM((row_count, 128), F32)],
        compiler_params=pltpu.CompilerParams(vmem_limit_bytes=4 * 2**20),
        name="finish",
    )(facts, prompt_terms, *resp_pieces)


def from_distance(block, distance):
    return lax.ppermute(block, "ctx", [(i, i ^ distance) for i in range(8)])


def meet(block):
    return jnp.concatenate([block, from_distance(block, 4)], axis=0)


def share(block):
    return [block] + [from_distance(block, distance) for distance in (3, 2, 1)][::-1]


def per_device(
    q_nope,
    q_rope,
    prompt_latent,
    prompt_rope,
    resp_latent,
    resp_rope,
    w_key,
    w_value,
    out_grad,
    lengths,
    offsets,
):
    ctx = lax.axis_index("ctx").astype(jnp.int32)
    core = jnp.bitwise_and(lax.axis_index("sample").astype(jnp.int32), 1)
    facts = jnp.concatenate([lengths, offsets, ctx[None], core[None]])
    same_core = [[2 * chip + c for chip in range(8)] for c in range(2)]
    w_own = lax.all_to_all(
        spread_weights(w_key, w_value, 8), "sample", 0, 0, tiled=True, axis_index_groups=same_core)
    prompt_pieces = share(meet(jnp.concatenate([prompt_latent, prompt_rope, prompt_rope], axis=1)))
    w_own, *prompt_pieces = lax.optimization_barrier((w_own, *prompt_pieces))
    w_other = lax.ppermute(w_own, "sample", [(i, i ^ 1) for i in range(16)])
    keys = join_keys(prompt_pieces, resp_latent, resp_rope)
    held = (q_nope, q_rope, out_grad, keys, w_own, w_other)
    terms, later_facts = lax.optimization_barrier((attention(True, facts, *held), facts))
    attn_out, grad_query_nope, grad_query_rope = attention(False, later_facts, *held)
    terms, attn_out, grad_query_nope, grad_query_rope = lax.optimization_barrier(
        (lax.all_to_all(terms, "ctx", 0, 0, tiled=True), attn_out, grad_query_nope, grad_query_rope))
    prompt_part, resp_part = add_heads(terms, 16)
    prompt_part = lax.all_to_all(prompt_part, "sample", 0, 0, tiled=True)
    resp_pieces = share(resp_part)
    prompt_lat, prompt_rot, resp_lat, resp_rot = finish(facts, prompt_part, resp_pieces)
    return (attn_out, grad_query_nope, grad_query_rope, prompt_lat, prompt_rot, resp_lat, resp_rot.T)


def solution(mesh):
    placed = (
        P(("group", "sample"), "ctx"),
        P(("group", "sample"), "ctx"),
        P(("group", "ctx"), None),
        P(("group", "ctx"), None),
        P(("group", "sample"), None),
        P(("group", "sample"), None),
        P("sample", "ctx"),
        P("sample", "ctx"),
        P(("group", "sample"), "ctx"),
        P(("group", "sample")),
        P(("group", "sample")),
    )
    return jax.shard_map(
        per_device,
        mesh=mesh,
        in_specs=placed,
        out_specs=(
            P(("group", "sample"), "ctx"),
            P(("group", "sample"), "ctx"),
            P(("group", "sample"), "ctx"),
            P(("group", "ctx"), None),
            P(("group", "ctx"), None),
            P(("group", "sample"), None),
            P(("group", "sample"), None),
        ),
        check_vma=False,
    )
```
